128 devices in a mesh: section: 2 (over y_lo), dp: 32 (over y_hi, z, x), mp: 2 (over core).
Axes of the slice: x: 4, y: 4 (y_hi: 2, y_lo: 2; y = y_hi * 2 + y_lo), z: 4, core: 2. Of those that a mesh axis runs over, the one named last changes fastest.
Arguments:
- inputs: bfloat16 [2, 32, 197, 768], P(None, 'dp'), may hold values from -6 to 6
- cotangent: bfloat16 [2, 32, 197, 768], P(None, 'dp'), may hold values from -6 to 6
- routes: int32 [2, 2, 32, 197, 2], P('section', None, 'dp'), may hold values from 0 to 3, all different within a row; in each aligned block of 197 rows (0 to 196, 197 to 393, ..., all dimensions but the last counted through in order) at most 128 rows name the same one
- gain_one: bfloat16 [2, 768], P('section', 'dp'), may hold values from 0.5 to 1.5
- shift_one: bfloat16 [2, 768], P('section', 'dp'), may hold values from -1 to 1
- qkv_weight: bfloat16 [2, 768, 3, 768], P('section', 'dp', None, 'mp'), may hold values from -0.3125 to 0.3125
- out_weight: bfloat16 [2, 768, 768], P('section', 'mp', 'dp'), may hold values from -0.75 to 0.75
- gain_two: bfloat16 [2, 768], P('section', 'dp'), may hold values from 0.5 to 1.5
- shift_two: bfloat16 [2, 768], P('section', 'dp'), may hold values from -1 to 1
- router: bfloat16 [2, 768, 4], P('section', 'dp'), may hold values from -0.15625 to 0.15625
- expert_in: bfloat16 [2, 4, 768, 3072], P('section', None, 'dp', 'mp'), may hold values from -0.21875 to 0.21875
- expert_out: bfloat16 [2, 4, 3072, 768], P('section', None, 'mp', 'dp'), may hold values from -0.4375 to 0.4375
Outputs:
- acts: bfloat16 [2, 2, 32, 197, 768], P('section', None, 'dp')
- input_grads: bfloat16 [2, 2, 32, 197, 768], P('section', None, 'dp')
- grad_gain_one: float32 [2, 768], P('section', 'dp')
- grad_shift_one: float32 [2, 768], P('section', 'dp')
- grad_qkv: float32 [2, 768, 3, 768], P('section', 'dp', None, 'mp')
- grad_out: float32 [2, 768, 768], P('section', 'mp', 'dp')
- grad_gain_two: float32 [2, 768], P('section', 'dp')
- grad_shift_two: float32 [2, 768], P('section', 'dp')
- grad_router: float32 [2, 768, 4], P('section', 'dp')
- grad_expert_in: float32 [2, 4, 768, 3072], P('section', None, 'dp', 'mp')
- grad_expert_out: float32 [2, 4, 3072, 768], P('section', None, 'mp', 'dp')
The draws below stay inside these ranges and needn't reach their ends.
Inputs may be any that keep to these rules, and one draw needn't show every extreme that they name: Each token names 2 different experts. Among the 197 tokens of one micro-batch in one group of 1 consecutive images, no expert is named by more than 128 routes, and in some groups one expert is named by exactly 128.
All inputs are finite; a program needn't handle non-finite values.
Results may differ from the reference program's by a relative error of at most 0.035.
Values may be sent and summed in bfloat16 or wider, within the bound.
No kernel may reach another device: no remote copies, remote signals or barrier semaphores. Data moves between devices by JAX's collectives and lax.ppermute only.
A program may use at most 256 MiB of HBM per device.

```python
import math
import jax
import jax.numpy as jnp
import numpy as np
from jax import lax

D = 768
HEADS = 12
HEAD_DIM = 64
FF = 3072
EXPERTS = 4
TOPK = 2
SEQ = 197
MICRO = 2
IMG = 1
IMAGES = 32
CAP = 128
N_SECTION = 2
N_DP = 32


def steps_of(stream_key, shape, cuts, low, high):
    def one(axis_at, shards_of):
        steps = jax.random.uniform(jax.random.fold_in(jax.random.fold_in(stream_key, 6), axis_at), (shards_of,), jnp.float32, low / len(cuts), high / len(cuts))
        return jnp.repeat(jnp.exp(steps), shape[axis_at] // shards_of).reshape((-1,) + (1,) * (len(shape) - axis_at - 1))

    factor_of = one(*cuts[0])
    for cut in cuts[1:]:
        factor_of = factor_of * one(*cut)
    return factor_of


def deal_out(stream_key, own, number, rows, amount, top, limit, slope):
    order = jax.random.permutation(stream_key, amount)
    packed, common = load_shares(amount, rows * top, limit, slope, True), load_shares(amount, rows * top, limit, slope, False)
    places = jnp.arange(amount)

    def named(tallies, rotation):
        used = int((tallies > 0).sum())
        fixed = max(1, used // 4)
        shifted = fixed + (places - fixed + rotation * (used - fixed)) % max(1, amount - fixed)
        return jnp.zeros((amount,), jnp.int32).at[order[jnp.where(places < fixed, places, shifted)]].set(jnp.asarray(tallies, jnp.int32))

    tallies = jnp.where(number % 4 == 0, named(packed, number // 4), named(common, number - number // 4 - 1))
    mixed = jax.random.permutation(jax.random.fold_in(own, 3), amount)
    giver, receiver = mixed[0:amount // 2 * 2:2], mixed[1:amount // 2 * 2:2]
    margin = jnp.minimum(tallies[giver] - 1, limit - tallies[receiver]) // 2
    margin = jnp.where((giver == order[0]) | (receiver == order[0]) | (tallies[receiver] == 0), 0, jnp.maximum(margin, 0))
    shifted = jax.random.randint(jax.random.fold_in(own, 4), (amount // 2,), 0, 1 << 20) % (margin + 1)
    tallies = tallies.at[giver].add(-shifted).at[receiver].add(shifted)
    items = jnp.searchsorted(jnp.cumsum(tallies), jnp.arange(rows * top), side="right").astype(jnp.int32)
    table = items.reshape(top, rows).T
    table = table[jax.random.permutation(jax.random.fold_in(own, 1), rows)]
    rotation = jax.random.randint(jax.random.fold_in(own, 2), (rows, 1), 0, top)
    return jnp.take_along_axis(table, (jnp.arange(top)[None, :] + rotation) % top, axis=1)


def load_shares(count, total, limit, slope, full):
    loads = [(1 << 20) // math.isqrt(rank ** slope) + 1 for rank in range(1, count + 1)]
    largest = limit if full else min(limit, max(-(-total // count), total * loads[0] // sum(loads)))
    least = 1 if total - largest >= count - 1 else 0
    holding, surplus = [largest] + [least] * (count - 1), total - largest - least * (count - 1)
    while surplus > 0:
        movable = [i for i in range(1, count) if holding[i] < largest] or [i for i in range(1, count) if holding[i] < limit]
        mass, remaining = sum([loads[i] for i in movable]), surplus
        for i in movable:
            addition = min(limit - holding[i], max(1, remaining * loads[i] // mass), surplus)
            holding[i] = holding[i] + addition
            surplus = surplus - addition
    return np.array(holding)


def centred(stream_key, shape, scale, reach, split=(), kind=jnp.bfloat16):
    entries = jax.random.normal(stream_key, shape, jnp.float32) * scale
    if len(split) > 0:
        entries = steps_of(stream_key, shape, split, -0.22, 0.18) * entries
    return jnp.clip(entries, min=-reach, max=reach).astype(kind)


def setup_inputs(seed: int = 0) -> dict:
    keys = jax.random.split(jax.random.key(seed), 13)
    inputs = centred(keys[0], (MICRO, IMAGES, SEQ, D), 1.0, 6.0, ((1, 32),))
    cotangent = centred(keys[1], (MICRO, IMAGES, SEQ, D), 1.0, 6.0, ((1, 32),))
    routes_keys = jax.random.split(jax.random.fold_in(keys[2], 1), N_SECTION * MICRO * IMAGES * SEQ // (IMG * SEQ))
    routes_turns = jax.random.permutation(jax.random.fold_in(keys[2], 3), N_SECTION * MICRO * IMAGES * SEQ // (IMG * SEQ))
    routes = jax.vmap(lambda own, number: deal_out(jax.random.fold_in(keys[2], 2), own, number, IMG * SEQ, EXPERTS, TOPK, CAP, 1))(routes_keys, routes_turns).reshape((N_SECTION, MICRO, IMAGES, SEQ, TOPK))
    gain_one = jnp.clip(1.0 + 0.1 * jax.random.normal(keys[3], (N_SECTION, D), jnp.float32), 0.5, 1.5).astype(jnp.bfloat16)
    shift_one = centred(keys[4], (N_SECTION, D), 0.2, 1.0, ((0, 2), (1, 32)))
    qkv_weight = centred(keys[5], (N_SECTION, D, 3, D), (D // 2) ** -0.5, 0.3125, ((0, 2), (1, 32), (3, 2)))
    out_weight = centred(keys[6], (N_SECTION, D, D), (max(D // 12, 4)) ** -0.5, 0.75, ((0, 2), (1, 2), (2, 32)))
    gain_two = jnp.clip(1.0 + 0.1 * jax.random.normal(keys[7], (N_SECTION, D), jnp.float32), 0.5, 1.5).astype(jnp.bfloat16)
    shift_two = centred(keys[8], (N_SECTION, D), 0.2, 1.0, ((0, 2), (1, 32)))
    router = centred(keys[9], (N_SECTION, D, EXPERTS), (2 * D) ** -0.5, 0.15625, ((0, 2), (1, 32)))
    expert_in = centred(keys[10], (N_SECTION, EXPERTS, D, FF), D ** -0.5, 0.21875, ((0, 2), (2, 32), (3, 2)))
    expert_out = centred(keys[11], (N_SECTION, EXPERTS, FF, D), (FF // 16) ** -0.5, 0.4375, ((0, 2), (2, 2), (3, 32)))
    return {"inputs": inputs, "cotangent": cotangent, "routes": routes, "gain_one": gain_one, "shift_one": shift_one, "qkv_weight": qkv_weight, "out_weight": out_weight, "gain_two": gain_two, "shift_two": shift_two, "router": router, "expert_in": expert_in, "expert_out": expert_out}


PRECISE = lax.Precision.HIGHEST
epsilon = 1e-06

@jax.custom_vjp
def low(v):
    return lax.optimization_barrier(v.astype(jnp.bfloat16)).astype(jnp.float32)

@jax.custom_vjp
def low_back(v):
    return v

def low_keep(v):
    return (low(v), None)

def low_pass(kept, grad):
    return (grad,)

def back_keep(v):
    return (v, None)

def back_low(kept, grad):
    return (low(grad),)
low.defvjp(low_keep, low_pass)
low_back.defvjp(back_keep, back_low)

def layer_norm(field, norm_gain, norm_shift):
    centered = field - lax.optimization_barrier(jnp.mean(field, axis=-1, keepdims=True))
    spread = lax.optimization_barrier(jnp.mean(centered * centered, axis=-1, keepdims=True))
    return centered * lax.rsqrt(spread + epsilon) * norm_gain + norm_shift

def route_slots(route_ids, capacity, experts):
    flattened = route_ids.reshape(-1)
    onehot = (flattened[:, None] == jnp.arange(experts, dtype=jnp.int32)[None, :]).astype(jnp.int32)
    before = jnp.cumsum(onehot, axis=0) - onehot
    position = lax.optimization_barrier(jnp.sum(before * onehot, axis=1))
    return (flattened * capacity + position).reshape(route_ids.shape)

def group_layer(params, tokens, route_ids):
    gain_one, shift_one, qkv_weight, out_weight, gain_two, shift_two, router, expert_in, expert_out = params
    token_count = tokens.shape[0]
    images = token_count // SEQ
    normed_one = low(layer_norm(tokens, gain_one, shift_one))
    projected = low_back(low(jnp.einsum('td,dcf->tcf', normed_one, qkv_weight, precision=PRECISE)))
    split_heads = projected.reshape(images, SEQ, 3, HEADS, HEAD_DIM)
    scores = low_back(jnp.einsum('bqhe,bkhe->bhqk', split_heads[:, :, 0], split_heads[:, :, 1], precision=PRECISE) * HEAD_DIM ** (-0.5))
    probability = low(jax.nn.softmax(scores, axis=-1))
    mixed_heads = low_back(low(jnp.einsum('bhqk,bkhe->bqhe', probability, split_heads[:, :, 2], precision=PRECISE)))
    mixed_heads = mixed_heads.reshape(token_count, HEADS * HEAD_DIM)
    hidden = tokens + low_back(jnp.dot(mixed_heads, out_weight, precision=PRECISE))
    normed_two = low(layer_norm(hidden, gain_two, shift_two))
    gate_probs = jax.nn.softmax(jnp.dot(normed_two, router, precision=PRECISE), axis=-1)
    chosen = jnp.take_along_axis(gate_probs, route_ids, axis=1)
    slot_ids = route_slots(route_ids, CAP, EXPERTS)
    select = (slot_ids[:, :, None] == jnp.arange(EXPERTS * CAP, dtype=jnp.int32)[None, None, :]).astype(jnp.float32)
    dispatched = jnp.einsum('tks,td->sd', select, normed_two, precision=PRECISE).reshape(EXPERTS, CAP, -1)
    inner_pre = low_back(jnp.einsum('ecd,edf->ecf', dispatched, expert_in, precision=PRECISE))
    activated = low(jax.nn.gelu(inner_pre, approximate=False))
    expert_sum = low_back(jnp.einsum('ecf,efd->ecd', activated, expert_out, precision=PRECISE)).reshape(EXPERTS * CAP, -1)
    picked = jnp.einsum('tks,sd->tkd', select, expert_sum, precision=PRECISE)
    return hidden + jnp.einsum('tk,tkd->td', chosen, picked, precision=PRECISE)

def apply_layer(params, stream, route_ids):
    groups = MICRO * N_DP
    tokens = stream.reshape(groups, IMG * SEQ, D)
    routed = route_ids.reshape(groups, IMG * SEQ, TOPK)
    group_step = jax.checkpoint(lambda group_pair: group_layer(params, group_pair[0], group_pair[1]))
    return lax.map(group_step, (tokens, routed)).reshape(stream.shape)

def reference(inputs, cotangent, routes, gain_one, shift_one, qkv_weight, out_weight, gain_two, shift_two, router, expert_in, expert_out):
    arrays = (gain_one, shift_one, qkv_weight, out_weight, gain_two, shift_two, router, expert_in, expert_out)
    params_first = tuple((member[0].astype(jnp.float32) for member in arrays))
    params_second = tuple((member[1].astype(jnp.float32) for member in arrays))
    first_out, back_first = jax.vjp(lambda params, stream: apply_layer(params, stream, routes[0]), params_first, inputs.astype(jnp.float32))
    middle = first_out.astype(jnp.bfloat16)
    last_out, back_second = jax.vjp(lambda params, stream: apply_layer(params, stream, routes[1]), params_second, middle.astype(jnp.float32))
    grads_second, middle_grad = back_second(cotangent.astype(jnp.float32))
    middle_low = middle_grad.astype(jnp.bfloat16)
    grads_first, input_grad = back_first(middle_low.astype(jnp.float32))
    acts = jnp.stack([middle, last_out.astype(jnp.bfloat16)])
    input_grads = jnp.stack([input_grad.astype(jnp.bfloat16), middle_low])
    stacked = [jnp.stack([first_part, second_part]) for first_part, second_part in zip(grads_first, grads_second)]
    return (acts, input_grads, stacked[0], stacked[1], stacked[2], stacked[3], stacked[4], stacked[5], stacked[6], stacked[7], stacked[8])
```

```python
import jax
import jax.numpy as jnp
from jax import lax
from jax.sharding import Mesh
from jax.sharding import PartitionSpec as P

HEAD_DIM = 64
SEQ = 197
CAP = 128
EPS = 1e-06
PRECISE = lax.Precision.HIGHEST
F32 = jnp.float32
BF16 = jnp.bfloat16


def dot(a, b, dims, precision=None):
    return lax.dot_general(a, b, (dims, ((), ())), precision=precision, preferred_element_type=F32)


def swap(block, axis, distance=1):
    size = lax.axis_size(axis)
    return lax.ppermute(block, axis, [(i, i ^ distance) for i in range(size)])


def send_one_way(block, axis, source, target):
    return lax.ppermute(block, axis, [(source, target)])


def piece(blocks, index):
    return lax.dynamic_index_in_dim(blocks, index, 0, keepdims=False)


def gathered(block, axis, place=0):
    size = lax.axis_size(axis)
    own = lax.axis_index(axis)
    shape = block.shape[:place] + (size,) + block.shape[place:]
    total = jnp.zeros(shape, block.dtype)
    for distance in range(size):
        arrived = block if distance == 0 else swap(block, axis, distance)
        total = lax.dynamic_update_slice_in_dim(
            total, jnp.expand_dims(arrived, place), own ^ distance, place
        )
    return total


def scattered(blocks, axis):
    size = lax.axis_size(axis)
    own = lax.axis_index(axis)
    total = piece(blocks, own).astype(F32)
    for distance in range(1, size):
        total = total + swap(piece(blocks, own ^ distance), axis, distance).astype(F32)
    return total


def exchanged(blocks, axis):
    size = lax.axis_size(axis)
    return [blocks[k] if k == 0 else swap(blocks[k], axis, k) for k in range(size)]


def xor_order(blocks, index):
    paired = blocks.reshape((2, 2) + blocks.shape[1:])
    paired = jnp.where((index & 1) == 1, paired[:, ::-1], paired)
    paired = jnp.where((index & 2) == 2, paired[::-1], paired)
    return paired.reshape(blocks.shape)


def normalise(field):
    centered = field - jnp.mean(field, axis=-1, keepdims=True)
    scale = lax.rsqrt(jnp.mean(centered * centered, axis=-1, keepdims=True) + EPS)
    return centered * scale, scale


def norm_back(grad, unit, scale, gain):
    grad_unit = grad * gain[None, :]
    mean_grad = jnp.mean(grad_unit, axis=-1, keepdims=True)
    mean_cross = jnp.mean(grad_unit * unit, axis=-1, keepdims=True)
    grad_field = scale * (grad_unit - mean_grad - unit * mean_cross)
    return grad_field, jnp.sum(grad * unit, axis=0), jnp.sum(grad, axis=0)


def slot_table(route_ids, axis_x, mp_index):
    experts = lax.axis_size("x")
    tokens = route_ids.shape[0]
    order = jnp.arange(experts, dtype=jnp.int32) ^ axis_x
    named = jnp.any(route_ids.T[None, :, :] == order[:, None, None], axis=1)
    steps = jnp.arange(tokens, dtype=jnp.int32)
    earlier = (steps[:, None] < steps[None, :]).astype(BF16)
    position = dot(named.astype(BF16), earlier, ((1,), (0,))).astype(jnp.int32)
    slots = jnp.arange(CAP // 2, dtype=jnp.int32) + mp_index * (CAP // 2)
    return named[:, None, :] & (position[:, None, :] == slots[None, :, None])


def to_experts(half):
    own = jnp.concatenate(exchanged(half, "x"), axis=0)
    return jnp.concatenate([own, swap(own, "mp")], axis=0)


def from_experts(partial, experts):
    rows = partial.shape[0] // 2
    other = swap(partial[rows:].astype(BF16), "mp")
    own = (partial[:rows] + other.astype(F32)).astype(BF16)
    own = own.reshape(experts, rows // experts, -1)
    return jnp.concatenate(exchanged(own, "x"), axis=0)


def forward_layer(dense, experts_pair, tokens, table, axis_x):
    qkv, out_t, gain_one, shift_one, gain_two, shift_two, router = dense
    first, second = experts_pair
    count, width = tokens.shape
    experts = table.shape[0]
    half_width = out_t.shape[1]
    heads = half_width // HEAD_DIM
    unit_one, scale_one = normalise(tokens)
    normed_one = (unit_one * gain_one[None, :] + shift_one[None, :]).astype(BF16)
    projected = dot(normed_one, qkv, ((1,), (0,))).astype(BF16)
    parts = projected.reshape(count, 3, heads, HEAD_DIM)
    queries, keys_all, values_all = parts[:, 0], parts[:, 1], parts[:, 2]
    scores = jnp.einsum(
        "qhe,khe->hqk", queries, keys_all, preferred_element_type=F32
    ) * HEAD_DIM ** (-0.5)
    probability = jax.nn.softmax(scores, axis=-1)
    prob_low = probability.astype(BF16)
    mixed = (
        jnp.einsum("hqk,khe->qhe", prob_low, values_all, preferred_element_type=F32)
        .astype(BF16)
        .reshape(count, half_width)
    )
    attended = dot(mixed, out_t, ((1,), (1,)))
    attended = attended + swap(attended, "mp")
    hidden = tokens + attended
    unit_two, scale_two = normalise(hidden)
    normed_two = (unit_two * gain_two[None, :] + shift_two[None, :]).astype(BF16)
    gates = jax.nn.softmax(dot(router, normed_two, ((0,), (1,))), axis=0)
    select = table.astype(BF16).reshape(-1, count)
    slot_gates = jnp.sum(jnp.where(table, gates[:, None, :], 0.0), axis=2).reshape(-1, 1)
    dispatched = to_experts(
        dot(select, normed_two, ((1,), (0,))).astype(BF16).reshape(experts, -1, width)
    )
    inner_pre = dot(dispatched, first, ((1,), (0,)))
    activated = jax.nn.gelu(inner_pre, approximate=False).astype(BF16)
    expert_sum = from_experts(dot(activated, second, ((1,), (1,))), experts)
    weighted = (slot_gates * expert_sum.astype(F32)).astype(BF16)
    mixture = dot(select, weighted, ((0,), (0,)))
    output = hidden + (mixture + swap(mixture, "mp"))
    saved = (
        unit_one,
        scale_one,
        normed_one,
        queries,
        keys_all,
        values_all,
        probability,
        prob_low,
        mixed,
        unit_two,
        scale_two,
        normed_two,
        gates,
        table,
        select,
        slot_gates,
        dispatched,
        inner_pre,
        activated,
        expert_sum,
    )
    return output.astype(BF16), saved


def backward_layer(dense, experts_pair, saved, grad_low):
    qkv, out_t, gain_one, shift_one, gain_two, shift_two, router = dense
    first, second = experts_pair
    (
        unit_one,
        scale_one,
        normed_one,
        queries,
        keys_all,
        values_all,
        probability,
        prob_low,
        mixed,
        unit_two,
        scale_two,
        normed_two,
        gates,
        table,
        select,
        slot_gates,
        dispatched,
        inner_pre,
        activated,
        expert_sum,
    ) = saved
    experts = table.shape[0]
    count, width = grad_low.shape
    grad_output = grad_low.astype(F32)
    grad_slots = dot(select, grad_low, ((1,), (0,)))
    slot_chosen = jnp.sum(grad_slots * expert_sum.astype(F32), axis=1).reshape(experts, -1, 1)
    grad_gates = jnp.sum(jnp.where(table, slot_chosen, 0.0), axis=1)
    grad_gates = grad_gates + swap(grad_gates, "mp")
    grad_expert = to_experts(
        (slot_gates * grad_slots).astype(BF16).reshape(experts, -1, width)
    )
    grad_act = dot(grad_expert, second, ((1,), (0,)))
    unused, gelu_back = jax.vjp(lambda field: jax.nn.gelu(field, approximate=False), inner_pre)
    grad_inner = gelu_back(grad_act)[0].astype(BF16)
    grad_dispatched = from_experts(dot(grad_inner, first, ((1,), (1,))), experts)
    grad_second = dot(grad_expert, activated, ((0,), (0,))).astype(BF16)
    grad_first = dot(dispatched, grad_inner, ((0,), (0,))).astype(BF16)
    returned = dot(select, grad_dispatched, ((0,), (0,)))
    returned = returned + swap(returned, "mp")
    grad_logits = gates * (grad_gates - jnp.sum(gates * grad_gates, axis=0, keepdims=True))
    grad_router = dot(normed_two.astype(F32), grad_logits, ((0,), (1,)), PRECISE)
    grad_normed = returned + dot(grad_logits, router.astype(F32), ((0,), (1,)), PRECISE)
    grad_hidden, grad_gain_two, grad_shift_two = norm_back(
        grad_normed, unit_two, scale_two, gain_two
    )
    grad_hidden = grad_output + grad_hidden
    grad_attended = grad_hidden.astype(BF16)
    grad_out_t = dot(grad_attended, mixed, ((0,), (0,)))
    grad_mixed = dot(grad_attended, out_t, ((1,), (0,))).astype(BF16).reshape(queries.shape)
    grad_prob = jnp.einsum("qhe,khe->hqk", grad_mixed, values_all, preferred_element_type=F32)
    grad_values = jnp.einsum("hqk,qhe->khe", prob_low, grad_mixed, preferred_element_type=F32)
    grad_scores = (
        probability * (grad_prob - jnp.sum(probability * grad_prob, axis=-1, keepdims=True))
    ).astype(BF16)
    grad_queries = jnp.einsum(
        "hqk,khe->qhe", grad_scores, keys_all, preferred_element_type=F32
    ) * HEAD_DIM ** (-0.5)
    grad_keys = jnp.einsum(
        "hqk,qhe->khe", grad_scores, queries, preferred_element_type=F32
    ) * HEAD_DIM ** (-0.5)
    grad_projected = (
        jnp.stack([grad_queries, grad_keys, grad_values], axis=1).astype(BF16).reshape(count, -1)
    )
    grad_qkv = dot(normed_one, grad_projected, ((0,), (0,)))
    grad_normed = dot(grad_projected, qkv, ((1,), (1,)))
    grad_normed = grad_normed + swap(grad_normed, "mp")
    grad_tokens, grad_gain_one, grad_shift_one = norm_back(
        grad_normed, unit_one, scale_one, gain_one
    )
    vectors = jnp.stack([grad_gain_one, grad_shift_one, grad_gain_two, grad_shift_two], axis=1)
    dense_grads = (grad_qkv, grad_out_t, vectors, grad_router)
    return (grad_hidden + grad_tokens).astype(BF16), dense_grads, (grad_first, grad_second)


def shards(
    inputs,
    cotangent,
    routes,
    gain_one,
    shift_one,
    qkv_weight,
    out_weight,
    gain_two,
    shift_two,
    router,
    expert_in,
    expert_out,
):
    section = lax.axis_index("section")
    axis_x = lax.axis_index("x")
    mp_index = lax.axis_index("mp")
    size_g = lax.axis_size("g")
    size_x = lax.axis_size("x")
    rows = qkv_weight.shape[1]
    width = rows * size_g * size_x
    half_width = out_weight.shape[1]
    first_section = section == 0

    def by_layer(own):
        other = swap(own, "section")
        return jnp.where(first_section, own, other), jnp.where(first_section, other, own)

    small = jnp.stack([gain_one[0], shift_one[0], gain_two[0], shift_two[0]], axis=1)
    attention_shard = qkv_weight[0].reshape(rows, 3 * half_width)
    rest_shard = jnp.concatenate(
        [out_weight[0].T, small, router[0], jnp.zeros((rows, 120), BF16)], axis=1
    )
    expert_shard = jnp.stack([expert_in[0], jnp.swapaxes(expert_out[0], 1, 2)], axis=1)
    attention_pair = by_layer(attention_shard)
    rest_pair = by_layer(rest_shard)
    expert_pair = by_layer(expert_shard)
    routes_own = routes[0, :, 0]
    routes_kept = piece(routes_own, section)
    routes_other = swap(piece(routes_own, 1 - section), "section")
    routes_pair = (
        jnp.where(first_section, routes_kept, routes_other),
        jnp.where(first_section, routes_other, routes_kept),
    )

    def dense_weights(layer):
        qkv = gathered(gathered(attention_pair[layer], "x"), "g").reshape(width, -1)
        rest = gathered(gathered(rest_pair[layer], "g"), "x", 1).reshape(width, -1)
        out_t = rest[:, :half_width]
        extra = rest[:, half_width : half_width + 8]
        vectors = extra[:, :4].astype(F32).T
        router_here = xor_order(extra[:, 4:].T, axis_x).T
        return (qkv, out_t, vectors[0], vectors[1], vectors[2], vectors[3], router_here)

    def expert_weights(layer):
        shard = expert_pair[layer]
        own = lax.axis_index("x")
        ordered = jnp.zeros((2, size_x) + shard.shape[2:], BF16)
        for distance in range(size_x):
            mine = piece(shard, own ^ distance)
            if distance > 0:
                mine = swap(mine, "x", distance)
            ordered = lax.dynamic_update_slice_in_dim(
                ordered, jnp.expand_dims(mine, 1), own ^ distance, 1
            )
        ordered = ordered.reshape(2, size_x * rows, -1)
        return tuple(
            (gathered(ordered[i], "g").reshape(width, -1) for i in range(2))
        )

    dense = (dense_weights(0), dense_weights(1))
    experts_here = (expert_weights(0), expert_weights(1))
    tables = tuple((slot_table(r, axis_x, mp_index) for r in routes_pair))
    tokens = piece(inputs[:, 0], section)
    out_zero, saved_zero = forward_layer(
        dense[0], experts_here[0], tokens.astype(F32), tables[0], axis_x
    )
    out_one, saved_one = forward_layer(
        dense[1], experts_here[1], out_zero.astype(F32), tables[1], axis_x
    )

    def by_section(zero, one):
        to_first = send_one_way(zero, "section", 1, 0)
        to_second = send_one_way(one, "section", 0, 1)
        low = jnp.where(first_section, zero, to_second)
        high = jnp.where(first_section, to_first, one)
        return jnp.stack([low, high])[None, :, None]

    acts = by_section(out_zero, out_one)

    def reduced_experts(layer, grads):
        first, second = grads
        parts = []
        for member in (first, second):
            parts.append(scattered(member.reshape(size_g, size_x * rows, -1), "g").astype(BF16))
        both = jnp.stack(parts).reshape(2, size_x, rows, -1)
        arrived = []
        for distance in range(size_x):
            mine = lax.dynamic_index_in_dim(both, axis_x ^ distance, 1, keepdims=False)
            arrived.append(mine if distance == 0 else swap(mine, "x", distance))
        arrived = xor_order(jnp.stack(arrived), axis_x)
        other = send_one_way(arrived, "section", 1 - layer, layer)
        return arrived.astype(F32) + other.astype(F32)

    def reduced_dense(layer, grads):
        grad_qkv, grad_out_t, vectors, grad_router = grads
        grad_router = xor_order(grad_router.T, axis_x).T
        rest = jnp.concatenate(
            [grad_out_t, vectors, grad_router, jnp.zeros((width, 120), F32)], axis=1
        ).astype(BF16)
        low = grad_qkv.astype(BF16).reshape(size_g, size_x * rows, -1)
        low = scattered(low, "g").astype(BF16)
        low = scattered(low.reshape(size_x, rows, -1), "x")
        rest = jnp.swapaxes(rest.reshape(size_g, size_x, rows, -1), 0, 1)
        rest = scattered(rest, "x").astype(BF16)
        rest = scattered(rest, "g")
        total = jnp.concatenate([low, rest], axis=1)
        other = send_one_way(total, "section", 1 - layer, layer)
        return total + other

    grad_mid, dense_one, expert_one = backward_layer(
        dense[1], experts_here[1], saved_one, piece(cotangent[:, 0], section)
    )
    experts_sum_one = reduced_experts(1, expert_one)
    dense_sum_one = reduced_dense(1, dense_one)
    grad_in, dense_zero, expert_zero = backward_layer(
        dense[0], experts_here[0], saved_zero, grad_mid
    )
    experts_sum_zero = reduced_experts(0, expert_zero)
    dense_sum_zero = reduced_dense(0, dense_zero)
    input_grads = by_section(grad_in, grad_mid)
    expert_sum = jnp.where(first_section, experts_sum_zero, experts_sum_one)
    dense_sum = jnp.where(first_section, dense_sum_zero, dense_sum_one)
    grad_first = expert_sum[:, 0]
    grad_second = jnp.swapaxes(expert_sum[:, 1], 1, 2)
    full = 3 * half_width
    grad_qkv = dense_sum[:, :full].reshape(rows, 3, half_width)
    grad_out = dense_sum[:, full : full + half_width].T
    tail = dense_sum[:, full + half_width :]
    outs = (
        tail[:, 0],
        tail[:, 1],
        grad_qkv,
        grad_out,
        tail[:, 2],
        tail[:, 3],
        tail[:, 4:8],
        grad_first,
        grad_second,
    )
    return (acts, input_grads) + tuple((member[None] for member in outs))


def solution(mesh):
    sections, batch, pair = mesh.devices.shape
    inner = Mesh(mesh.devices.reshape(sections, batch // 4, 4, pair), ("section", "g", "x", "mp"))
    dp = ("g", "x")
    placed = (
        P(None, dp, None, None),
        P(None, dp, None, None),
        P("section", None, dp, None, None),
        P("section", dp),
        P("section", dp),
        P("section", dp, None, "mp"),
        P("section", "mp", dp),
        P("section", dp),
        P("section", dp),
        P("section", dp, None),
        P("section", None, dp, "mp"),
        P("section", None, "mp", dp),
    )
    return jax.shard_map(
        shards,
        mesh=inner,
        in_specs=placed,
        out_specs=(
            P("section", None, dp, None, None),
            P("section", None, dp, None, None),
            P("section", dp),
            P("section", dp),
            P("section", dp, None, "mp"),
            P("section", "mp", dp),
            P("section", dp),
            P("section", dp),
            P("section", dp, None),
            P("section", None, dp, "mp"),
            P("section", None, "mp", dp),
        ),
        check_vma=False,
    )
```

```python
import jax
import jax.numpy as jnp
from jax import lax
from jax.sharding import Mesh
from jax.sharding import PartitionSpec as P

HEAD_DIM = 64
SEQ = 197
CAP = 128
EPS = 1e-06
PRECISE = lax.Precision.HIGHEST
F32 = jnp.float32
BF16 = jnp.bfloat16


def dot(a, b, dims, precision=None):
    return lax.dot_general(a, b, (dims, ((), ())), precision=precision, preferred_element_type=F32)


def swap(block, axis, distance=1):
    size = lax.axis_size(axis)
    return lax.ppermute(block, axis, [(i, i ^ distance) for i in range(size)])


def piece(blocks, index):
    return lax.dynamic_index_in_dim(blocks, index, 0, keepdims=False)


def all_to_all(blocks, axis):
    return lax.all_to_all(blocks, axis, 0, 0, tiled=True)


def summed(blocks):
    return jnp.sum(blocks.astype(F32), axis=0)


def normalise(field):
    centered = field - jnp.mean(field, axis=-1, keepdims=True)
    scale = lax.rsqrt(jnp.mean(centered * centered, axis=-1, keepdims=True) + EPS)
    return centered * scale, scale


def norm_back(grad, unit, scale, gain):
    grad_unit = grad * gain[None, :]
    mean_grad = jnp.mean(grad_unit, axis=-1, keepdims=True)
    mean_cross = jnp.mean(grad_unit * unit, axis=-1, keepdims=True)
    grad_field = scale * (grad_unit - mean_grad - unit * mean_cross)
    return grad_field, jnp.sum(grad * unit, axis=0), jnp.sum(grad, axis=0)


def slot_table(route_ids, mp_index):
    tokens = route_ids.shape[0]
    order = jnp.arange(lax.axis_size("x"), dtype=jnp.int32)
    named = jnp.any(route_ids.T[None, :, :] == order[:, None, None], axis=1)
    steps = jnp.arange(tokens, dtype=jnp.int32)
    earlier = (steps[:, None] < steps[None, :]).astype(BF16)
    position = dot(named.astype(BF16), earlier, ((1,), (0,))).astype(jnp.int32)
    slots = jnp.arange(CAP // 2, dtype=jnp.int32) + mp_index * (CAP // 2)
    return named[:, None, :] & (position[:, None, :] == slots[None, :, None])


def to_experts(half):
    own = all_to_all(half, "x").reshape(-1, half.shape[2])
    return jnp.concatenate([own, swap(own, "mp")], axis=0)


def from_experts(partial, experts):
    rows = partial.shape[0] // 2
    other = swap(partial[rows:].astype(BF16), "mp")
    own = (partial[:rows] + other.astype(F32)).astype(BF16)
    own = own.reshape(experts, rows // experts, -1)
    return all_to_all(own, "x").reshape(rows, -1)


def forward_layer(dense, experts_pair, tokens, table, beside):
    qkv, out_t, gain_one, shift_one, gain_two, shift_two, router = dense
    first, second = experts_pair[0], experts_pair[1]
    count, width = tokens.shape
    experts = table.shape[0]
    half_width = out_t.shape[1]
    heads = half_width // HEAD_DIM
    unit_one, scale_one = normalise(tokens)
    normed_one = (unit_one * gain_one[None, :] + shift_one[None, :]).astype(BF16)
    projected = dot(normed_one, qkv, ((1,), (0,))).astype(BF16)
    parts = projected.reshape(count, 3, heads, HEAD_DIM)
    queries, keys_all, values_all = parts[:, 0], parts[:, 1], parts[:, 2]
    scores = jnp.einsum(
        "qhe,khe->hqk", queries, keys_all, preferred_element_type=F32
    ) * HEAD_DIM ** (-0.5)
    probability = jax.nn.softmax(scores, axis=-1)
    prob_low = probability.astype(BF16)
    mixed = (
        jnp.einsum("hqk,khe->qhe", prob_low, values_all, preferred_element_type=F32)
        .astype(BF16)
        .reshape(count, half_width)
    )
    attended = dot(mixed, out_t, ((1,), (1,)))
    attended = attended + swap(attended, "mp")
    hidden = tokens + attended
    unit_two, scale_two = normalise(hidden)
    normed_two = (unit_two * gain_two[None, :] + shift_two[None, :]).astype(BF16)
    gates = jax.nn.softmax(dot(router, normed_two, ((0,), (1,))), axis=0)
    select = table.astype(BF16).reshape(-1, count)
    slot_gates = jnp.sum(jnp.where(table, gates[:, None, :], 0.0), axis=2).reshape(-1, 1)
    dispatched = to_experts(
        dot(select, normed_two, ((1,), (0,))).astype(BF16).reshape(experts, -1, width)
    )
    if beside is not None:
        dispatched, beside = lax.optimization_barrier((dispatched, beside))
    inner_pre = dot(dispatched, first, ((1,), (0,)))
    below = 0.5 * (1.0 + lax.erf(inner_pre * 0.5**0.5))
    activated = (inner_pre * below).astype(BF16)
    expert_sum = from_experts(dot(activated, second, ((1,), (1,))), experts)
    weighted = (slot_gates * expert_sum.astype(F32)).astype(BF16)
    mixture = dot(select, weighted, ((0,), (0,)))
    output = hidden + (mixture + swap(mixture, "mp"))
    saved = (
        unit_one,
        scale_one,
        normed_one,
        queries,
        keys_all,
        values_all,
        probability,
        prob_low,
        mixed,
        unit_two,
        scale_two,
        normed_two,
        gates,
        table,
        select,
        slot_gates,
        dispatched,
        inner_pre,
        below,
        activated,
        expert_sum,
    )
    return output.astype(BF16), saved, beside


def together(value, others):
    joined = lax.optimization_barrier((value,) + tuple(others))
    return joined[0], joined[1:]


def backward_layer(dense, experts_pair, saved, grad_low, pack, early, late):
    qkv, out_t, gain_one, shift_one, gain_two, shift_two, router = dense
    first, second = experts_pair[0], experts_pair[1]
    (
        unit_one,
        scale_one,
        normed_one,
        queries,
        keys_all,
        values_all,
        probability,
        prob_low,
        mixed,
        unit_two,
        scale_two,
        normed_two,
        gates,
        table,
        select,
        slot_gates,
        dispatched,
        inner_pre,
        below,
        activated,
        expert_sum,
    ) = saved
    experts = table.shape[0]
    count, width = grad_low.shape
    grad_output = grad_low.astype(F32)
    grad_slots = dot(select, grad_low, ((1,), (0,)))
    slot_chosen = jnp.sum(grad_slots * expert_sum.astype(F32), axis=1).reshape(experts, -1, 1)
    grad_gates = jnp.sum(jnp.where(table, slot_chosen, 0.0), axis=1)
    grad_gates = grad_gates + swap(grad_gates, "mp")
    grad_expert = to_experts(
        (slot_gates * grad_slots).astype(BF16).reshape(experts, -1, width)
    )
    if pack is not None:
        grad_expert, (pack,) = together(grad_expert, (pack,))
        pack = all_to_all(pack, "x")
    grad_act = dot(grad_expert, second, ((1,), (0,)))
    density = jnp.exp(-0.5 * inner_pre * inner_pre) * (2.0 * 3.141592653589793) ** -0.5
    grad_inner = (grad_act * (below + inner_pre * density)).astype(BF16)
    grad_second = dot(grad_expert, activated, ((0,), (0,))).astype(BF16)
    grad_first = dot(dispatched, grad_inner, ((0,), (0,))).astype(BF16)
    grad_rows = dot(grad_inner, first, ((1,), (1,)))
    if pack is not None:
        grad_rows, (pack,) = together(grad_rows, (pack,))
    grad_dispatched = from_experts(grad_rows, experts)
    pair = jnp.stack([grad_first, grad_second])
    grad_dispatched, (pair, *early) = together(grad_dispatched, (pair,) + early)
    expert_grads = lax.psum_scatter(pair, "g", scatter_dimension=1, tiled=True)
    returned = dot(select, grad_dispatched, ((0,), (0,)))
    returned = returned + swap(returned, "mp")
    grad_logits = gates * (grad_gates - jnp.sum(gates * grad_gates, axis=0, keepdims=True))
    grad_router = dot(normed_two.astype(F32), grad_logits, ((0,), (1,)), PRECISE)
    grad_normed = returned + dot(grad_logits, router.astype(F32), ((0,), (1,)), PRECISE)
    grad_hidden, grad_gain_two, grad_shift_two = norm_back(
        grad_normed, unit_two, scale_two, gain_two
    )
    grad_hidden = grad_output + grad_hidden
    grad_attended = grad_hidden.astype(BF16)
    grad_out_t = dot(grad_attended, mixed, ((0,), (0,)))
    grad_mixed = dot(grad_attended, out_t, ((1,), (0,))).astype(BF16).reshape(queries.shape)
    grad_prob = jnp.einsum("qhe,khe->hqk", grad_mixed, values_all, preferred_element_type=F32)
    grad_values = jnp.einsum("hqk,qhe->khe", prob_low, grad_mixed, preferred_element_type=F32)
    grad_scores = (
        probability * (grad_prob - jnp.sum(probability * grad_prob, axis=-1, keepdims=True))
    ).astype(BF16)
    grad_queries = jnp.einsum(
        "hqk,khe->qhe", grad_scores, keys_all, preferred_element_type=F32
    ) * HEAD_DIM ** (-0.5)
    grad_keys = jnp.einsum(
        "hqk,qhe->khe", grad_scores, queries, preferred_element_type=F32
    ) * HEAD_DIM ** (-0.5)
    grad_projected = (
        jnp.stack([grad_queries, grad_keys, grad_values], axis=1).astype(BF16).reshape(count, -1)
    )
    if late:
        grad_projected, late = together(grad_projected, late)
    grad_qkv = dot(normed_one, grad_projected, ((0,), (0,)))
    grad_normed = dot(grad_projected, qkv, ((1,), (1,)))
    grad_normed = grad_normed + swap(grad_normed, "mp")
    grad_tokens, grad_gain_one, grad_shift_one = norm_back(
        grad_normed, unit_one, scale_one, gain_one
    )
    vectors = jnp.stack([grad_gain_one, grad_shift_one, grad_gain_two, grad_shift_two], axis=1)
    dense_grads = (grad_qkv, grad_out_t, vectors, grad_router)
    grad_low = (grad_hidden + grad_tokens).astype(BF16)
    return grad_low, dense_grads, expert_grads, pack, early, late


def shards(
    inputs,
    cotangent,
    routes,
    gain_one,
    shift_one,
    qkv_weight,
    out_weight,
    gain_two,
    shift_two,
    router,
    expert_in,
    expert_out,
):
    section = lax.axis_index("section")
    mp_index = lax.axis_index("mp")
    size_g = lax.axis_size("g")
    size_x = lax.axis_size("x")
    rows = qkv_weight.shape[1]
    width = rows * size_g * size_x
    half_width = out_weight.shape[1]
    first_section = section == 0

    def by_layer(own):
        other = swap(own, "section")
        return jnp.where(first_section, own, other), jnp.where(first_section, other, own)

    small = jnp.stack([gain_one[0], shift_one[0], gain_two[0], shift_two[0]], axis=1)
    dense_shard = jnp.concatenate(
        [
            qkv_weight[0].reshape(rows, 3 * half_width),
            out_weight[0].T,
            small,
            router[0],
            jnp.zeros((rows, 120), BF16),
        ],
        axis=1,
    )
    expert_shard = jnp.stack([expert_in[0], jnp.swapaxes(expert_out[0], 1, 2)], axis=1)
    routes_own = routes[0, :, 0]
    routes_kept = piece(routes_own, section)
    routes_other = swap(piece(routes_own, 1 - section), "section")
    routes_pair = (
        jnp.where(first_section, routes_kept, routes_other),
        jnp.where(first_section, routes_other, routes_kept),
    )

    full = 3 * half_width

    expert_own = all_to_all(expert_shard, "x")
    expert_own = jnp.swapaxes(expert_own, 0, 1).reshape(2, size_x * rows, -1)
    both = jnp.stack(by_layer(dense_shard))
    both = all_to_all(jnp.broadcast_to(both[None], (size_g,) + both.shape), "g")

    def gathered(layer):
        block = both[:, layer]
        block = all_to_all(jnp.broadcast_to(block[None], (size_x,) + block.shape), "x")
        return jnp.swapaxes(block, 0, 1).reshape(width, -1)

    def dense_weights(pack):
        extra = pack[:, full + half_width : full + half_width + 8]
        vectors = extra[:, :4].astype(F32).T
        return (
            pack[:, :full],
            pack[:, full : full + half_width],
            vectors[0],
            vectors[1],
            vectors[2],
            vectors[3],
            extra[:, 4:],
        )

    expert_all = lax.all_gather(expert_own, ("section", "g"), axis=0, tiled=False)
    expert_all = expert_all.reshape(2, size_g, 2, size_x * rows, -1)
    experts_here = tuple(
        (
            tuple((expert_all[layer, :, i].reshape(width, -1) for i in range(2)))
            for layer in range(2)
        )
    )
    pack_zero = gathered(0)
    pack_one = gathered(1)
    dense_zero = dense_weights(pack_zero)
    tables = tuple((slot_table(r, mp_index) for r in routes_pair))
    tokens = piece(inputs[:, 0], section)
    out_zero, saved_zero, pack_one = forward_layer(
        dense_zero, experts_here[0], tokens.astype(F32), tables[0], pack_one
    )
    dense_one = dense_weights(pack_one)
    out_one, saved_one, unused = forward_layer(
        dense_one, experts_here[1], out_zero.astype(F32), tables[1], None
    )

    def by_section(zero, one):
        own = jnp.where(first_section, zero, one)
        other = swap(jnp.where(first_section, one, zero), "section")
        low = jnp.where(first_section, own, other)
        high = jnp.where(first_section, other, own)
        return jnp.stack([low, high])[None, :, None]

    def section_sum(zero, one):
        own = jnp.where(first_section, zero, one)
        other = swap(jnp.where(first_section, one, zero), "section")
        return own.astype(F32) + other.astype(F32)

    acts = by_section(out_zero, out_one)

    def owned_experts(own):
        own = own.astype(BF16).reshape(2, size_x, rows, -1)
        return all_to_all(jnp.swapaxes(own, 0, 1), "x")

    def packed(grads):
        pack = jnp.concatenate(list(grads) + [jnp.zeros((width, 120), F32)], axis=1)
        return jnp.swapaxes(pack.astype(BF16).reshape(size_g, size_x, rows, -1), 0, 1)

    grad_mid, grads_one, expert_one, unused, (acts,), unused = backward_layer(
        dense_one, experts_here[1], saved_one, piece(cotangent[:, 0], section), None, (acts,), ()
    )
    grad_in, grads_zero, expert_zero, pack_one, unused, late = backward_layer(
        dense_zero,
        experts_here[0],
        saved_zero,
        grad_mid,
        packed(grads_one),
        (),
        (owned_experts(expert_one),),
    )
    pack_zero = all_to_all(packed(grads_zero), "x")
    dense_both = jnp.stack([summed(pack_zero), summed(pack_one)], axis=1).astype(BF16)
    dense_both = summed(all_to_all(dense_both, "g"))
    dense_sum = section_sum(dense_both[0], dense_both[1])
    expert_sum = section_sum(owned_experts(expert_zero), late[0])
    input_grads = by_section(grad_in, grad_mid)
    grad_first = expert_sum[:, 0]
    grad_second = jnp.swapaxes(expert_sum[:, 1], 1, 2)
    grad_qkv = dense_sum[:, :full].reshape(rows, 3, half_width)
    grad_out = dense_sum[:, full : full + half_width].T
    tail = dense_sum[:, full + half_width :]
    outs = (
        tail[:, 0],
        tail[:, 1],
        grad_qkv,
        grad_out,
        tail[:, 2],
        tail[:, 3],
        tail[:, 4:8],
        grad_first,
        grad_second,
    )
    return (acts, input_grads) + tuple((member[None] for member in outs))


def solution(mesh):
    sections, batch, pair = mesh.devices.shape
    inner = Mesh(mesh.devices.reshape(sections, batch // 4, 4, pair), ("section", "g", "x", "mp"))
    dp = ("g", "x")
    placed = (
        P(None, dp, None, None),
        P(None, dp, None, None),
        P("section", None, dp, None, None),
        P("section", dp),
        P("section", dp),
        P("section", dp, None, "mp"),
        P("section", "mp", dp),
        P("section", dp),
        P("section", dp),
        P("section", dp, None),
        P("section", None, dp, "mp"),
        P("section", None, "mp", dp),
    )
    return jax.shard_map(
        shards,
        mesh=inner,
        in_specs=placed,
        out_specs=(
            P("section", None, dp, None, None),
            P("section", None, dp, None, None),
            P("section", dp),
            P("section", dp),
            P("section", dp, None, "mp"),
            P("section", "mp", dp),
            P("section", dp),
            P("section", dp),
            P("section", dp, None),
            P("section", None, dp, "mp"),
            P("section", None, "mp", dp),
        ),
        check_vma=False,
    )
```

```python
import jax
import jax.numpy as jnp
from jax import lax
from jax.sharding import Mesh
from jax.sharding import PartitionSpec as P

HEAD_DIM = 64
SEQ = 197
CAP = 128
EPS = 1e-06
PRECISE = lax.Precision.HIGHEST
F32 = jnp.float32
BF16 = jnp.bfloat16


def dot(a, b, dims, precision=None):
    return lax.dot_general(a, b, (dims, ((), ())), precision=precision, preferred_element_type=F32)


def swap(block, axis, distance=1):
    size = lax.axis_size(axis)
    return lax.ppermute(block, axis, [(i, i ^ distance) for i in range(size)])


def piece(blocks, index):
    return lax.dynamic_index_in_dim(blocks, index, 0, keepdims=False)


def all_to_all(blocks, axis):
    return lax.all_to_all(blocks, axis, 0, 0, tiled=True)


def summed(blocks):
    return jnp.sum(blocks.astype(F32), axis=0)


def xor_order(blocks, index):
    paired = blocks.reshape((2, 2) + blocks.shape[1:])
    paired = jnp.where((index & 1) == 1, paired[:, ::-1], paired)
    paired = jnp.where((index & 2) == 2, paired[::-1], paired)
    return paired.reshape(blocks.shape)


def by_owner(grad):
    size_g, size_x = lax.axis_size("g"), lax.axis_size("x")
    blocks = grad.astype(BF16).reshape(size_g, size_x, -1, grad.shape[1])
    return jnp.swapaxes(blocks, 0, 1)


def normalise(field):
    centered = field - jnp.mean(field, axis=-1, keepdims=True)
    scale = lax.rsqrt(jnp.mean(centered * centered, axis=-1, keepdims=True) + EPS)
    return centered * scale, scale


def norm_back(grad, unit, scale, gain):
    grad_unit = grad * gain[None, :]
    mean_grad = jnp.mean(grad_unit, axis=-1, keepdims=True)
    mean_cross = jnp.mean(grad_unit * unit, axis=-1, keepdims=True)
    grad_field = scale * (grad_unit - mean_grad - unit * mean_cross)
    return grad_field, jnp.sum(grad * unit, axis=0), jnp.sum(grad, axis=0)


def slot_table(route_ids, mp_index):
    tokens = route_ids.shape[0]
    order = jnp.arange(lax.axis_size("x"), dtype=jnp.int32)
    named = jnp.any(route_ids.T[None, :, :] == order[:, None, None], axis=1)
    steps = jnp.arange(tokens, dtype=jnp.int32)
    earlier = (steps[:, None] < steps[None, :]).astype(BF16)
    position = dot(named.astype(BF16), earlier, ((1,), (0,))).astype(jnp.int32)
    slots = jnp.arange(CAP // 2, dtype=jnp.int32) + mp_index * (CAP // 2)
    return named[:, None, :] & (position[:, None, :] == slots[None, :, None])


def to_experts(half):
    own = all_to_all(half, "x").reshape(-1, half.shape[2])
    return jnp.concatenate([own, swap(own, "mp")], axis=0)


def from_experts(partial, experts):
    rows = partial.shape[0] // 2
    other = swap(partial[rows:].astype(BF16), "mp")
    own = (partial[:rows] + other.astype(F32)).astype(BF16)
    own = own.reshape(experts, rows // experts, -1)
    return all_to_all(own, "x").reshape(rows, -1)


def forward_layer(dense, experts_pair, tokens, table, beside):
    qkv, out_t, gain_one, shift_one, gain_two, shift_two, router = dense
    first, second = experts_pair[0], experts_pair[1]
    count, width = tokens.shape
    experts = table.shape[0]
    half_width = out_t.shape[1]
    heads = half_width // HEAD_DIM
    unit_one, scale_one = normalise(tokens)
    normed_one = (unit_one * gain_one[None, :] + shift_one[None, :]).astype(BF16)
    projected = dot(normed_one, qkv, ((1,), (0,))).astype(BF16)
    parts = projected.reshape(count, 3, heads, HEAD_DIM)
    queries, keys_all, values_all = parts[:, 0], parts[:, 1], parts[:, 2]
    scores = jnp.einsum(
        "qhe,khe->hqk", queries, keys_all, preferred_element_type=F32
    ) * HEAD_DIM ** (-0.5)
    probability = jax.nn.softmax(scores, axis=-1)
    prob_low = probability.astype(BF16)
    mixed = (
        jnp.einsum("hqk,khe->qhe", prob_low, values_all, preferred_element_type=F32)
        .astype(BF16)
        .reshape(count, half_width)
    )
    attended = dot(mixed, out_t, ((1,), (1,)))
    attended = attended + swap(attended, "mp")
    hidden = tokens + attended
    unit_two, scale_two = normalise(hidden)
    normed_two = (unit_two * gain_two[None, :] + shift_two[None, :]).astype(BF16)
    gates = jax.nn.softmax(dot(router, normed_two, ((0,), (1,))), axis=0)
    select = table.astype(BF16).reshape(-1, count)
    slot_gates = jnp.sum(jnp.where(table, gates[:, None, :], 0.0), axis=2).reshape(-1, 1)
    dispatched = to_experts(
        dot(select, normed_two, ((1,), (0,))).astype(BF16).reshape(experts, -1, width)
    )
    if beside is not None:
        dispatched, beside = lax.optimization_barrier((dispatched, beside))
    inner_pre = dot(dispatched, first, ((1,), (0,)))
    below = 0.5 * (1.0 + lax.erf(inner_pre * 0.5**0.5))
    activated = (inner_pre * below).astype(BF16)
    expert_sum = from_experts(dot(activated, second, ((1,), (1,))), experts)
    weighted = (slot_gates * expert_sum.astype(F32)).astype(BF16)
    mixture = dot(select, weighted, ((0,), (0,)))
    output = hidden + (mixture + swap(mixture, "mp"))
    saved = (
        unit_one,
        scale_one,
        normed_one,
        queries,
        keys_all,
        values_all,
        probability,
        prob_low,
        mixed,
        unit_two,
        scale_two,
        normed_two,
        gates,
        table,
        select,
        slot_gates,
        dispatched,
        inner_pre,
        below,
        activated,
        expert_sum,
    )
    return output.astype(BF16), saved, beside


def together(value, others):
    joined = lax.optimization_barrier((value,) + tuple(others))
    return joined[0], joined[1:]


def backward_layer(dense, experts_pair, saved, grad_low, pack, early, late):
    qkv, out_t, gain_one, shift_one, gain_two, shift_two, router = dense
    first, second = experts_pair[0], experts_pair[1]
    (
        unit_one,
        scale_one,
        normed_one,
        queries,
        keys_all,
        values_all,
        probability,
        prob_low,
        mixed,
        unit_two,
        scale_two,
        normed_two,
        gates,
        table,
        select,
        slot_gates,
        dispatched,
        inner_pre,
        below,
        activated,
        expert_sum,
    ) = saved
    experts = table.shape[0]
    count, width = grad_low.shape
    grad_output = grad_low.astype(F32)
    grad_slots = dot(select, grad_low, ((1,), (0,)))
    slot_chosen = jnp.sum(grad_slots * expert_sum.astype(F32), axis=1).reshape(experts, -1, 1)
    grad_gates = jnp.sum(jnp.where(table, slot_chosen, 0.0), axis=1)
    grad_gates = grad_gates + swap(grad_gates, "mp")
    grad_expert = to_experts(
        (slot_gates * grad_slots).astype(BF16).reshape(experts, -1, width)
    )
    grad_act = dot(grad_expert, second, ((1,), (0,)))
    density = jnp.exp(-0.5 * inner_pre * inner_pre) * (2.0 * 3.141592653589793) ** -0.5
    grad_inner = (grad_act * (below + inner_pre * density)).astype(BF16)
    grad_second = dot(grad_expert, activated, ((0,), (0,))).astype(BF16)
    grad_first = dot(dispatched, grad_inner, ((0,), (0,))).astype(BF16)
    grad_rows = dot(grad_inner, first, ((1,), (1,)))
    grad_dispatched = from_experts(grad_rows, experts)
    pair = jnp.stack([grad_first, grad_second])
    if pack is not None:
        early = early + (pack,)
    grad_dispatched, (pair, *early) = together(grad_dispatched, (pair,) + early)
    if pack is not None:
        pack = all_to_all(early.pop(), "x")
    expert_grads = lax.psum_scatter(pair, "g", scatter_dimension=1, tiled=True)
    returned = dot(select, grad_dispatched, ((0,), (0,)))
    returned = returned + swap(returned, "mp")
    grad_logits = gates * (grad_gates - jnp.sum(gates * grad_gates, axis=0, keepdims=True))
    grad_router = dot(normed_two.astype(F32), grad_logits, ((0,), (1,)), PRECISE)
    grad_normed = returned + dot(grad_logits, router.astype(F32), ((0,), (1,)), PRECISE)
    grad_hidden, grad_gain_two, grad_shift_two = norm_back(
        grad_normed, unit_two, scale_two, gain_two
    )
    grad_hidden = grad_output + grad_hidden
    blank = jnp.zeros((width, 124), BF16)
    grad_attended = grad_hidden.astype(BF16)
    grad_out_t = dot(grad_attended, mixed, ((0,), (0,)))
    grad_mixed = dot(grad_attended, out_t, ((1,), (0,))).astype(BF16).reshape(queries.shape)
    grad_prob = jnp.einsum("qhe,khe->hqk", grad_mixed, values_all, preferred_element_type=F32)
    grad_values = jnp.einsum("hqk,qhe->khe", prob_low, grad_mixed, preferred_element_type=F32)
    grad_scores = (
        probability * (grad_prob - jnp.sum(probability * grad_prob, axis=-1, keepdims=True))
    ).astype(BF16)
    grad_queries = jnp.einsum(
        "hqk,khe->qhe", grad_scores, keys_all, preferred_element_type=F32
    ) * HEAD_DIM ** (-0.5)
    grad_keys = jnp.einsum(
        "hqk,qhe->khe", grad_scores, queries, preferred_element_type=F32
    ) * HEAD_DIM ** (-0.5)
    grad_projected = (
        jnp.stack([grad_queries, grad_keys, grad_values], axis=1).astype(BF16).reshape(count, -1)
    )
    if pack is not None:
        rest = (grad_out_t, jnp.stack([grad_gain_two, grad_shift_two], axis=1), grad_router)
        rest = jnp.concatenate([part.astype(BF16) for part in rest + (blank[:, 2:],)], axis=1)
        rest, (pack,) = together(by_owner(rest), (pack,))
        rest = all_to_all(rest, "x")
        grad_projected, (rest, *late) = together(grad_projected, (rest,) + late)
    grad_qkv = dot(normed_one, grad_projected, ((0,), (0,)))
    grad_normed = dot(grad_projected, qkv, ((1,), (1,)))
    grad_normed = grad_normed + swap(grad_normed, "mp")
    grad_tokens, grad_gain_one, grad_shift_one = norm_back(
        grad_normed, unit_one, scale_one, gain_one
    )
    ones = jnp.stack([grad_gain_one, grad_shift_one], axis=1)
    if pack is not None:
        dense_grads = (all_to_all(by_owner(grad_qkv), "x"), rest, ones)
    else:
        twos = jnp.stack([grad_gain_two, grad_shift_two], axis=1)
        dense_grads = (grad_qkv, grad_out_t, ones, twos, grad_router, blank[:, 4:])
    grad_low = (grad_hidden + grad_tokens).astype(BF16)
    return grad_low, dense_grads, expert_grads, pack, early, late


def shards(
    inputs,
    cotangent,
    routes,
    gain_one,
    shift_one,
    qkv_weight,
    out_weight,
    gain_two,
    shift_two,
    router,
    expert_in,
    expert_out,
):
    section = lax.axis_index("section")
    mp_index = lax.axis_index("mp")
    size_g = lax.axis_size("g")
    size_x = lax.axis_size("x")
    rows = qkv_weight.shape[1]
    width = rows * size_g * size_x
    half_width = out_weight.shape[1]
    first_section = section == 0

    def by_layer(own):
        other = swap(own, "section")
        return jnp.where(first_section, own, other), jnp.where(first_section, other, own)

    small = jnp.stack([gain_one[0], shift_one[0], gain_two[0], shift_two[0]], axis=1)
    dense_shard = jnp.concatenate(
        [
            qkv_weight[0].reshape(rows, 3 * half_width),
            out_weight[0].T,
            small,
            router[0],
            jnp.zeros((rows, 120), BF16),
        ],
        axis=1,
    )
    expert_shard = jnp.stack([expert_in[0], jnp.swapaxes(expert_out[0], 1, 2)], axis=1)
    routes_own = routes[0, :, 0]
    routes_kept = piece(routes_own, section)
    routes_other = swap(piece(routes_own, 1 - section), "section")
    routes_pair = (
        jnp.where(first_section, routes_kept, routes_other),
        jnp.where(first_section, routes_other, routes_kept),
    )

    full = 3 * half_width

    expert_own = all_to_all(expert_shard, "x")
    expert_own = jnp.swapaxes(expert_own, 0, 1).reshape(2, size_x * rows, -1)
    both = jnp.stack(by_layer(dense_shard))
    both = all_to_all(jnp.broadcast_to(both[None], (size_g,) + both.shape), "g")

    def gathered(layer):
        block = both[:, layer]
        block = all_to_all(jnp.broadcast_to(block[None], (size_x,) + block.shape), "x")
        return jnp.swapaxes(block, 0, 1).reshape(width, -1)

    def dense_weights(pack):
        extra = pack[:, full + half_width : full + half_width + 8]
        vectors = extra[:, :4].astype(F32).T
        return (
            pack[:, :full],
            pack[:, full : full + half_width],
            vectors[0],
            vectors[1],
            vectors[2],
            vectors[3],
            extra[:, 4:],
        )

    expert_all = lax.all_gather(expert_own, ("section", "g"), axis=1, tiled=True)
    experts_here = (expert_all[:, :width], expert_all[:, width:])
    pack_zero = gathered(0)
    pack_one = gathered(1)
    dense_zero = dense_weights(pack_zero)
    tables = tuple((slot_table(r, mp_index) for r in routes_pair))
    tokens = piece(inputs[:, 0], section)
    out_zero, saved_zero, pack_one = forward_layer(
        dense_zero, experts_here[0], tokens.astype(F32), tables[0], pack_one
    )
    dense_one = dense_weights(pack_one)
    out_one, saved_one, unused = forward_layer(
        dense_one, experts_here[1], out_zero.astype(F32), tables[1], None
    )

    def by_section(zero, one):
        own = jnp.where(first_section, zero, one)
        other = swap(jnp.where(first_section, one, zero), "section")
        low = jnp.where(first_section, own, other)
        high = jnp.where(first_section, other, own)
        return jnp.stack([low, high])[None, :, None]

    def section_sum(zero, one):
        own = jnp.where(first_section, zero, one)
        other = swap(jnp.where(first_section, one, zero), "section")
        return own.astype(F32) + other.astype(F32)

    acts = by_section(out_zero, out_one)

    axis_x = lax.axis_index("x")

    def owned_experts(own):
        own = jnp.swapaxes(own.reshape(2, size_x, rows, -1), 0, 1)
        arrived = [piece(own, axis_x)]
        for distance in range(1, size_x):
            arrived.append(swap(piece(own, axis_x ^ distance), "x", distance))
        return xor_order(jnp.stack(arrived), axis_x)

    grad_mid, grads_one, expert_one, unused, (acts,), unused = backward_layer(
        dense_one, experts_here[1], saved_one, piece(cotangent[:, 0], section), None, (acts,), ()
    )
    grad_in, grads_zero, expert_zero, pack_one, unused, late = backward_layer(
        dense_zero,
        experts_here[0],
        saved_zero,
        grad_mid,
        by_owner(jnp.concatenate([part.astype(BF16) for part in grads_one], axis=1)),
        (),
        (owned_experts(expert_one),),
    )
    qkv_zero, rest_zero, ones_zero = grads_zero
    ones_zero = by_owner(ones_zero).reshape(size_x, -1, rows * 2)
    total = piece(ones_zero, axis_x).astype(F32)
    for distance in range(1, size_x):
        arrived = swap(piece(ones_zero, axis_x ^ distance), "x", distance)
        total = total + arrived.astype(F32)
    ones_zero = total.reshape(size_g, rows, 2)
    qkv_zero, rest_zero = summed(qkv_zero), summed(rest_zero)
    dense_zero_sum = jnp.concatenate(
        [
            qkv_zero,
            rest_zero[:, :, :half_width],
            ones_zero,
            rest_zero[:, :, half_width:-2],
        ],
        axis=2,
    )
    dense_both = jnp.stack([dense_zero_sum, summed(pack_one)], axis=1).astype(BF16)
    dense_both = summed(all_to_all(dense_both, "g"))
    dense_sum = section_sum(dense_both[0], dense_both[1])
    expert_sum = section_sum(owned_experts(expert_zero), late[0])
    input_grads = by_section(grad_in, grad_mid)
    grad_first = expert_sum[:, 0]
    grad_second = jnp.swapaxes(expert_sum[:, 1], 1, 2)
    grad_qkv = dense_sum[:, :full].reshape(rows, 3, half_width)
    grad_out = dense_sum[:, full : full + half_width].T
    tail = dense_sum[:, full + half_width :]
    outs = (
        tail[:, 0],
        tail[:, 1],
        grad_qkv,
        grad_out,
        tail[:, 2],
        tail[:, 3],
        tail[:, 4:8],
        grad_first,
        grad_second,
    )
    return (acts, input_grads) + tuple((member[None] for member in outs))


def solution(mesh):
    sections, batch, pair = mesh.devices.shape
    inner = Mesh(mesh.devices.reshape(sections, batch // 4, 4, pair), ("section", "g", "x", "mp"))
    dp = ("g", "x")
    placed = (
        P(None, dp, None, None),
        P(None, dp, None, None),
        P("section", None, dp, None, None),
        P("section", dp),
        P("section", dp),
        P("section", dp, None, "mp"),
        P("section", "mp", dp),
        P("section", dp),
        P("section", dp),
        P("section", dp, None),
        P("section", None, dp, "mp"),
        P("section", None, "mp", dp),
    )
    return jax.shard_map(
        shards,
        mesh=inner,
        in_specs=placed,
        out_specs=(
            P("section", None, dp, None, None),
            P("section", None, dp, None, None),
            P("section", dp),
            P("section", dp),
            P("section", dp, None, "mp"),
            P("section", "mp", dp),
            P("section", dp),
            P("section", dp),
            P("section", dp, None),
            P("section", None, dp, "mp"),
            P("section", None, "mp", dp),
        ),
        check_vma=False,
    )
```

```python
import jax
import jax.numpy as jnp
from jax import lax
from jax.sharding import Mesh
from jax.sharding import PartitionSpec as P

HEAD_DIM = 64
SEQ = 197
CAP = 128
EPS = 1e-06
PRECISE = lax.Precision.HIGHEST
F32 = jnp.float32
BF16 = jnp.bfloat16


def dot(a, b, dims, precision=None):
    return lax.dot_general(a, b, (dims, ((), ())), precision=precision, preferred_element_type=F32)


def swap(block, axis, distance=1):
    size = lax.axis_size(axis)
    return lax.ppermute(block, axis, [(i, i ^ distance) for i in range(size)])


def piece(blocks, index):
    return lax.dynamic_index_in_dim(blocks, index, 0, keepdims=False)


def all_to_all(blocks, axis):
    return lax.all_to_all(blocks, axis, 0, 0, tiled=True)


def summed(blocks):
    return jnp.sum(blocks.astype(F32), axis=0)


def xor_order(blocks, index):
    paired = blocks.reshape((2, 2) + blocks.shape[1:])
    paired = jnp.where((index & 1) == 1, paired[:, ::-1], paired)
    paired = jnp.where((index & 2) == 2, paired[::-1], paired)
    return paired.reshape(blocks.shape)


def by_owner(grad):
    size_g, size_x = lax.axis_size("g"), lax.axis_size("x")
    blocks = grad.astype(BF16).reshape(size_g, size_x, -1, grad.shape[1])
    return jnp.swapaxes(blocks, 0, 1)


def normalise(field):
    centered = field - jnp.mean(field, axis=-1, keepdims=True)
    scale = lax.rsqrt(jnp.mean(centered * centered, axis=-1, keepdims=True) + EPS)
    return centered * scale, scale


def norm_back(grad, unit, scale, gain):
    grad_unit = grad * gain[None, :]
    mean_grad = jnp.mean(grad_unit, axis=-1, keepdims=True)
    mean_cross = jnp.mean(grad_unit * unit, axis=-1, keepdims=True)
    grad_field = scale * (grad_unit - mean_grad - unit * mean_cross)
    return grad_field, jnp.sum(grad * unit, axis=0), jnp.sum(grad, axis=0)


def slot_table(route_ids, mp_index):
    tokens = route_ids.shape[0]
    order = jnp.arange(lax.axis_size("x"), dtype=jnp.int32)
    named = jnp.any(route_ids.T[None, :, :] == order[:, None, None], axis=1)
    steps = jnp.arange(tokens, dtype=jnp.int32)
    earlier = (steps[:, None] < steps[None, :]).astype(BF16)
    position = dot(named.astype(BF16), earlier, ((1,), (0,))).astype(jnp.int32)
    slots = jnp.arange(CAP // 2, dtype=jnp.int32) + mp_index * (CAP // 2)
    return named[:, None, :] & (position[:, None, :] == slots[None, :, None])


def to_experts(half):
    own = all_to_all(half, "x").reshape(-1, half.shape[2])
    return jnp.concatenate([own, swap(own, "mp")], axis=0)


def from_experts(partial, experts):
    rows = partial.shape[0] // 2
    other = swap(partial[rows:].astype(BF16), "mp")
    own = (partial[:rows] + other.astype(F32)).astype(BF16)
    own = own.reshape(experts, rows // experts, -1)
    return all_to_all(own, "x").reshape(rows, -1)


def forward_layer(dense, experts_pair, tokens, table, beside):
    qkv, out_t, gain_one, shift_one, gain_two, shift_two, router = dense
    first, second = experts_pair[0], experts_pair[1]
    count, width = tokens.shape
    experts = table.shape[0]
    half_width = out_t.shape[1]
    heads = half_width // HEAD_DIM
    unit_one, scale_one = normalise(tokens)
    normed_one = (unit_one * gain_one[None, :] + shift_one[None, :]).astype(BF16)
    projected = dot(normed_one, qkv, ((1,), (0,))).astype(BF16)
    parts = projected.reshape(count, 3, heads, HEAD_DIM)
    queries, keys_all, values_all = parts[:, 0], parts[:, 1], parts[:, 2]
    scores = jnp.einsum(
        "qhe,khe->hqk", queries, keys_all, preferred_element_type=F32
    ) * HEAD_DIM ** (-0.5)
    probability = jax.nn.softmax(scores, axis=-1)
    prob_low = probability.astype(BF16)
    mixed = (
        jnp.einsum("hqk,khe->qhe", prob_low, values_all, preferred_element_type=F32)
        .astype(BF16)
        .reshape(count, half_width)
    )
    attended = dot(mixed, out_t, ((1,), (1,)))
    attended = attended + swap(attended, "mp")
    hidden = tokens + attended
    unit_two, scale_two = normalise(hidden)
    normed_two = (unit_two * gain_two[None, :] + shift_two[None, :]).astype(BF16)
    gates = jax.nn.softmax(dot(router, normed_two, ((0,), (1,))), axis=0)
    select = table.astype(BF16).reshape(-1, count)
    slot_gates = jnp.sum(jnp.where(table, gates[:, None, :], 0.0), axis=2).reshape(-1, 1)
    dispatched = to_experts(
        dot(select, normed_two, ((1,), (0,))).astype(BF16).reshape(experts, -1, width)
    )
    if beside is not None:
        dispatched, beside = lax.optimization_barrier((dispatched, beside))
    inner_pre = dot(dispatched, first, ((1,), (0,)))
    below = 0.5 * (1.0 + lax.erf(inner_pre * 0.5**0.5))
    activated = (inner_pre * below).astype(BF16)
    expert_sum = from_experts(dot(activated, second, ((1,), (1,))), experts)
    weighted = (slot_gates * expert_sum.astype(F32)).astype(BF16)
    mixture = dot(select, weighted, ((0,), (0,)))
    output = hidden + (mixture + swap(mixture, "mp"))
    saved = (
        unit_one,
        scale_one,
        normed_one,
        queries,
        keys_all,
        values_all,
        probability,
        prob_low,
        mixed,
        unit_two,
        scale_two,
        normed_two,
        gates,
        table,
        select,
        slot_gates,
        dispatched,
        inner_pre,
        below,
        activated,
        expert_sum,
    )
    return output.astype(BF16), saved, beside


def together(value, others):
    joined = lax.optimization_barrier((value,) + tuple(others))
    return joined[0], joined[1:]


def backward_layer(dense, experts_pair, saved, grad_low, pack, early, late):
    qkv, out_t, gain_one, shift_one, gain_two, shift_two, router = dense
    first, second = experts_pair[0], experts_pair[1]
    (
        unit_one,
        scale_one,
        normed_one,
        queries,
        keys_all,
        values_all,
        probability,
        prob_low,
        mixed,
        unit_two,
        scale_two,
        normed_two,
        gates,
        table,
        select,
        slot_gates,
        dispatched,
        inner_pre,
        below,
        activated,
        expert_sum,
    ) = saved
    experts = table.shape[0]
    count, width = grad_low.shape
    grad_output = grad_low.astype(F32)
    grad_slots = dot(select, grad_low, ((1,), (0,)))
    slot_chosen = jnp.sum(grad_slots * expert_sum.astype(F32), axis=1).reshape(experts, -1, 1)
    grad_gates = jnp.sum(jnp.where(table, slot_chosen, 0.0), axis=1)
    grad_gates = grad_gates + swap(grad_gates, "mp")
    grad_expert = to_experts(
        (slot_gates * grad_slots).astype(BF16).reshape(experts, -1, width)
    )
    grad_act = dot(grad_expert, second, ((1,), (0,)))
    density = jnp.exp(-0.5 * inner_pre * inner_pre) * (2.0 * 3.141592653589793) ** -0.5
    grad_inner = (grad_act * (below + inner_pre * density)).astype(BF16)
    grad_second = dot(grad_expert, activated, ((0,), (0,))).astype(BF16)
    grad_first = dot(dispatched, grad_inner, ((0,), (0,))).astype(BF16)
    grad_rows = dot(grad_inner, first, ((1,), (1,)))
    grad_dispatched = from_experts(grad_rows, experts)
    pair = jnp.stack([grad_first, grad_second])
    if pack is not None:
        early = early + (pack,)
    grad_dispatched, (pair, *early) = together(grad_dispatched, (pair,) + early)
    if pack is not None:
        pack = all_to_all(early.pop(), "x")
    expert_grads = lax.psum_scatter(pair, "g", scatter_dimension=1, tiled=True)
    returned = dot(select, grad_dispatched, ((0,), (0,)))
    returned = returned + swap(returned, "mp")
    grad_logits = gates * (grad_gates - jnp.sum(gates * grad_gates, axis=0, keepdims=True))
    grad_router = dot(normed_two.astype(F32), grad_logits, ((0,), (1,)), PRECISE)
    grad_normed = returned + dot(grad_logits, router.astype(F32), ((0,), (1,)), PRECISE)
    grad_hidden, grad_gain_two, grad_shift_two = norm_back(
        grad_normed, unit_two, scale_two, gain_two
    )
    grad_hidden = grad_output + grad_hidden
    blank = jnp.zeros((width, 124), BF16)
    grad_attended = grad_hidden.astype(BF16)
    grad_out_t = dot(grad_attended, mixed, ((0,), (0,)))
    grad_mixed = dot(grad_attended, out_t, ((1,), (0,))).astype(BF16).reshape(queries.shape)
    grad_prob = jnp.einsum("qhe,khe->hqk", grad_mixed, values_all, preferred_element_type=F32)
    grad_values = jnp.einsum("hqk,qhe->khe", prob_low, grad_mixed, preferred_element_type=F32)
    grad_scores = (
        probability * (grad_prob - jnp.sum(probability * grad_prob, axis=-1, keepdims=True))
    ).astype(BF16)
    grad_queries = jnp.einsum(
        "hqk,khe->qhe", grad_scores, keys_all, preferred_element_type=F32
    ) * HEAD_DIM ** (-0.5)
    grad_keys = jnp.einsum(
        "hqk,qhe->khe", grad_scores, queries, preferred_element_type=F32
    ) * HEAD_DIM ** (-0.5)
    grad_projected = (
        jnp.stack([grad_queries, grad_keys, grad_values], axis=1).astype(BF16).reshape(count, -1)
    )
    if pack is not None:
        rest = (grad_out_t, jnp.stack([grad_gain_two, grad_shift_two], axis=1), grad_router)
        rest = jnp.concatenate([part.astype(BF16) for part in rest + (blank[:, 2:],)], axis=1)
        rest, (pack,) = together(by_owner(rest), (pack,))
        rest = all_to_all(rest, "x")
        grad_projected, (rest, *late) = together(grad_projected, (rest,) + late)
    grad_qkv = dot(normed_one, grad_projected, ((0,), (0,)))
    grad_normed = dot(grad_projected, qkv, ((1,), (1,)))
    grad_normed = grad_normed + swap(grad_normed, "mp")
    grad_tokens, grad_gain_one, grad_shift_one = norm_back(
        grad_normed, unit_one, scale_one, gain_one
    )
    ones = jnp.stack([grad_gain_one, grad_shift_one], axis=1)
    if pack is not None:
        dense_grads = (all_to_all(by_owner(grad_qkv), "x"), rest, ones)
    else:
        twos = jnp.stack([grad_gain_two, grad_shift_two], axis=1)
        dense_grads = (grad_qkv, grad_out_t, ones, twos, grad_router, blank[:, 4:])
    grad_low = (grad_hidden + grad_tokens).astype(BF16)
    return grad_low, dense_grads, expert_grads, pack, early, late


def shards(
    inputs,
    cotangent,
    routes,
    gain_one,
    shift_one,
    qkv_weight,
    out_weight,
    gain_two,
    shift_two,
    router,
    expert_in,
    expert_out,
):
    section = lax.axis_index("section")
    mp_index = lax.axis_index("mp")
    size_g = lax.axis_size("g")
    size_x = lax.axis_size("x")
    rows = qkv_weight.shape[1]
    width = rows * size_g * size_x
    half_width = out_weight.shape[1]
    first_section = section == 0

    def by_layer(own):
        other = swap(own, "section")
        return jnp.where(first_section, own, other), jnp.where(first_section, other, own)

    small = jnp.stack([gain_one[0], shift_one[0], gain_two[0], shift_two[0]], axis=1)
    dense_shard = jnp.concatenate(
        [
            qkv_weight[0].reshape(rows, 3 * half_width),
            out_weight[0].T,
            small,
            router[0],
            jnp.zeros((rows, 120), BF16),
        ],
        axis=1,
    )
    expert_shard = jnp.stack([expert_in[0], jnp.swapaxes(expert_out[0], 1, 2)], axis=1)
    routes_own = routes[0, :, 0]
    routes_kept = piece(routes_own, section)
    routes_other = swap(piece(routes_own, 1 - section), "section")
    routes_pair = (
        jnp.where(first_section, routes_kept, routes_other),
        jnp.where(first_section, routes_other, routes_kept),
    )

    full = 3 * half_width

    expert_own = all_to_all(expert_shard, "x")
    expert_own = jnp.swapaxes(expert_own, 0, 1).reshape(2, size_x * rows, -1)
    both = jnp.stack(by_layer(dense_shard))
    both = all_to_all(jnp.broadcast_to(both[None], (size_g,) + both.shape), "g")

    def gathered(layer):
        block = both[:, layer]
        block = all_to_all(jnp.broadcast_to(block[None], (size_x,) + block.shape), "x")
        return jnp.swapaxes(block, 0, 1).reshape(width, -1)

    def dense_weights(pack):
        extra = pack[:, full + half_width : full + half_width + 8]
        vectors = extra[:, :4].astype(F32).T
        return (
            pack[:, :full],
            pack[:, full : full + half_width],
            vectors[0],
            vectors[1],
            vectors[2],
            vectors[3],
            extra[:, 4:],
        )

    own_zero, own_one = by_layer(expert_own)
    pack_zero, (own_one,) = together(gathered(0), (own_one,))
    experts_here = tuple(
        (lax.all_gather(own, "g", axis=1, tiled=True) for own in (own_zero, own_one))
    )
    pack_one = gathered(1)
    dense_zero = dense_weights(pack_zero)
    tables = tuple((slot_table(r, mp_index) for r in routes_pair))
    tokens = piece(inputs[:, 0], section)
    out_zero, saved_zero, pack_one = forward_layer(
        dense_zero, experts_here[0], tokens.astype(F32), tables[0], pack_one
    )
    dense_one = dense_weights(pack_one)
    out_one, saved_one, unused = forward_layer(
        dense_one, experts_here[1], out_zero.astype(F32), tables[1], None
    )

    def traded(zero, one):
        own = jnp.where(first_section, zero, one)
        return own, swap(jnp.where(first_section, one, zero), "section")

    def stacked(own, other):
        low = jnp.where(first_section, own, other)
        high = jnp.where(first_section, other, own)
        return jnp.stack([low, high])[None, :, None]

    acts = stacked(*traded(out_zero, out_one))

    axis_x = lax.axis_index("x")

    def owned_experts(own):
        own = jnp.swapaxes(own.reshape(2, size_x, rows, -1), 0, 1)
        arrived = [piece(own, axis_x)]
        for distance in range(1, size_x):
            arrived.append(swap(piece(own, axis_x ^ distance), "x", distance))
        return xor_order(jnp.stack(arrived), axis_x)

    grad_mid, grads_one, expert_one, unused, (acts,), unused = backward_layer(
        dense_one, experts_here[1], saved_one, piece(cotangent[:, 0], section), None, (acts,), ()
    )
    grad_in, grads_zero, expert_zero, pack_one, unused, late = backward_layer(
        dense_zero,
        experts_here[0],
        saved_zero,
        grad_mid,
        by_owner(jnp.concatenate([part.astype(BF16) for part in grads_one], axis=1)),
        (),
        (owned_experts(expert_one),),
    )
    qkv_zero, rest_zero, ones_zero = grads_zero
    ones_zero = by_owner(ones_zero).reshape(size_x, -1, rows * 2)
    total = piece(ones_zero, axis_x).astype(F32)
    for distance in range(1, size_x):
        arrived = swap(piece(ones_zero, axis_x ^ distance), "x", distance)
        total = total + arrived.astype(F32)
    ones_zero = total.reshape(size_g, rows, 2)
    qkv_zero, rest_zero = summed(qkv_zero), summed(rest_zero)
    dense_zero_sum = jnp.concatenate(
        [
            qkv_zero,
            rest_zero[:, :, :half_width],
            ones_zero,
            rest_zero[:, :, half_width:-2],
        ],
        axis=2,
    )
    dense_both = jnp.stack([dense_zero_sum, summed(pack_one)], axis=1).astype(BF16)
    dense_both = summed(all_to_all(dense_both, "g"))
    dense_own, dense_other = traded(dense_both[0], dense_both[1])
    expert_own, expert_other = traded(owned_experts(expert_zero), late[0])
    grads_own, grads_other = traded(grad_in, grad_mid)
    expert_other, (dense_other, grads_other) = together(expert_other, (dense_other, grads_other))
    input_grads = stacked(grads_own, grads_other)
    dense_sum = dense_own + dense_other
    expert_sum = expert_own.astype(F32) + expert_other.astype(F32)
    grad_first = expert_sum[:, 0]
    grad_second = jnp.swapaxes(expert_sum[:, 1], 1, 2)
    grad_qkv = dense_sum[:, :full].reshape(rows, 3, half_width)
    grad_out = dense_sum[:, full : full + half_width].T
    tail = dense_sum[:, full + half_width :]
    outs = (
        tail[:, 0],
        tail[:, 1],
        grad_qkv,
        grad_out,
        tail[:, 2],
        tail[:, 3],
        tail[:, 4:8],
        grad_first,
        grad_second,
    )
    return (acts, input_grads) + tuple((member[None] for member in outs))


def solution(mesh):
    sections, batch, pair = mesh.devices.shape
    inner = Mesh(mesh.devices.reshape(sections, batch // 4, 4, pair), ("section", "g", "x", "mp"))
    dp = ("g", "x")
    placed = (
        P(None, dp, None, None),
        P(None, dp, None, None),
        P("section", None, dp, None, None),
        P("section", dp),
        P("section", dp),
        P("section", dp, None, "mp"),
        P("section", "mp", dp),
        P("section", dp),
        P("section", dp),
        P("section", dp, None),
        P("section", None, dp, "mp"),
        P("section", None, "mp", dp),
    )
    return jax.shard_map(
        shards,
        mesh=inner,
        in_specs=placed,
        out_specs=(
            P("section", None, dp, None, None),
            P("section", None, dp, None, None),
            P("section", dp),
            P("section", dp),
            P("section", dp, None, "mp"),
            P("section", "mp", dp),
            P("section", dp),
            P("section", dp),
            P("section", dp, None),
            P("section", None, dp, "mp"),
            P("section", None, "mp", dp),
        ),
        check_vma=False,
    )
```

```python
import jax
import jax.numpy as jnp
from jax import lax
from jax.sharding import Mesh
from jax.sharding import PartitionSpec as P

HEAD_DIM = 64
SEQ = 197
CAP = 128
EPS = 1e-06
PRECISE = lax.Precision.HIGHEST
F32 = jnp.float32
BF16 = jnp.bfloat16


def dot(a, b, dims, precision=None):
    return lax.dot_general(a, b, (dims, ((), ())), precision=precision, preferred_element_type=F32)


def swap(block, axis, distance=1):
    size = lax.axis_size(axis)
    return lax.ppermute(block, axis, [(i, i ^ distance) for i in range(size)])


def piece(blocks, index):
    return lax.dynamic_index_in_dim(blocks, index, 0, keepdims=False)


def all_to_all(blocks, axis):
    return lax.all_to_all(blocks, axis, 0, 0, tiled=True)


def summed(blocks):
    return jnp.sum(blocks.astype(F32), axis=0)


def xor_order(blocks, index):
    paired = blocks.reshape((2, 2) + blocks.shape[1:])
    paired = jnp.where((index & 1) == 1, paired[:, ::-1], paired)
    paired = jnp.where((index & 2) == 2, paired[::-1], paired)
    return paired.reshape(blocks.shape)


def by_owner(grad):
    size_g, size_x = lax.axis_size("g"), lax.axis_size("x")
    blocks = grad.astype(BF16).reshape(size_g, size_x, -1, grad.shape[1])
    return jnp.swapaxes(blocks, 0, 1)


def normalise(field):
    centered = field - jnp.mean(field, axis=-1, keepdims=True)
    scale = lax.rsqrt(jnp.mean(centered * centered, axis=-1, keepdims=True) + EPS)
    return centered * scale, scale


def norm_back(grad, unit, scale, gain):
    grad_unit = grad * gain[None, :]
    mean_grad = jnp.mean(grad_unit, axis=-1, keepdims=True)
    mean_cross = jnp.mean(grad_unit * unit, axis=-1, keepdims=True)
    grad_field = scale * (grad_unit - mean_grad - unit * mean_cross)
    return grad_field, jnp.sum(grad * unit, axis=0), jnp.sum(grad, axis=0)


def slot_table(route_ids, mp_index):
    tokens = route_ids.shape[0]
    order = jnp.arange(lax.axis_size("x"), dtype=jnp.int32)
    named = jnp.any(route_ids.T[None, :, :] == order[:, None, None], axis=1)
    steps = jnp.arange(tokens, dtype=jnp.int32)
    earlier = (steps[:, None] < steps[None, :]).astype(BF16)
    position = dot(named.astype(BF16), earlier, ((1,), (0,))).astype(jnp.int32)
    slots = jnp.arange(CAP // 2, dtype=jnp.int32) + mp_index * (CAP // 2)
    return named[:, None, :] & (position[:, None, :] == slots[None, :, None])


def to_experts(half):
    own = all_to_all(half, "x").reshape(-1, half.shape[2])
    return jnp.concatenate([own, swap(own, "mp")], axis=0)


def from_experts(partial, experts):
    rows = partial.shape[0] // 2
    other = swap(partial[rows:].astype(BF16), "mp")
    own = (partial[:rows] + other.astype(F32)).astype(BF16)
    own = own.reshape(experts, rows // experts, -1)
    return all_to_all(own, "x").reshape(rows, -1)


def forward_layer(dense, experts_pair, tokens, table, beside):
    qkv, out_t, gain_one, shift_one, gain_two, shift_two, router = dense
    first, second = experts_pair[0], experts_pair[1]
    count, width = tokens.shape
    experts = table.shape[0]
    half_width = out_t.shape[1]
    heads = half_width // HEAD_DIM
    unit_one, scale_one = normalise(tokens)
    normed_one = (unit_one * gain_one[None, :] + shift_one[None, :]).astype(BF16)
    projected = dot(normed_one, qkv, ((1,), (0,))).astype(BF16)
    parts = projected.reshape(count, 3, heads, HEAD_DIM)
    queries, keys_all, values_all = parts[:, 0], parts[:, 1], parts[:, 2]
    scores = jnp.einsum(
        "qhe,khe->hqk", queries, keys_all, preferred_element_type=F32
    ) * HEAD_DIM ** (-0.5)
    probability = jax.nn.softmax(scores, axis=-1)
    prob_low = probability.astype(BF16)
    mixed = (
        jnp.einsum("hqk,khe->qhe", prob_low, values_all, preferred_element_type=F32)
        .astype(BF16)
        .reshape(count, half_width)
    )
    attended = dot(mixed, out_t, ((1,), (1,)))
    attended = attended + swap(attended, "mp")
    hidden = tokens + attended
    unit_two, scale_two = normalise(hidden)
    normed_two = (unit_two * gain_two[None, :] + shift_two[None, :]).astype(BF16)
    gates = jax.nn.softmax(dot(router, normed_two, ((0,), (1,))), axis=0)
    select = table.astype(BF16).reshape(-1, count)
    slot_gates = jnp.sum(jnp.where(table, gates[:, None, :], 0.0), axis=2).reshape(-1, 1)
    dispatched = to_experts(
        dot(select, normed_two, ((1,), (0,))).astype(BF16).reshape(experts, -1, width)
    )
    if beside is not None:
        dispatched, beside = lax.optimization_barrier((dispatched, beside))
    inner_pre = dot(dispatched, first, ((1,), (0,)))
    below = 0.5 * (1.0 + lax.erf(inner_pre * 0.5**0.5))
    activated = (inner_pre * below).astype(BF16)
    expert_sum = from_experts(dot(activated, second, ((1,), (1,))), experts)
    weighted = (slot_gates * expert_sum.astype(F32)).astype(BF16)
    mixture = dot(select, weighted, ((0,), (0,)))
    output = hidden + (mixture + swap(mixture, "mp"))
    saved = (
        unit_one,
        scale_one,
        normed_one,
        queries,
        keys_all,
        values_all,
        probability,
        prob_low,
        mixed,
        unit_two,
        scale_two,
        normed_two,
        gates,
        table,
        select,
        slot_gates,
        dispatched,
        inner_pre,
        below,
        activated,
        expert_sum,
    )
    return output.astype(BF16), saved, beside


def together(value, others):
    joined = lax.optimization_barrier((value,) + tuple(others))
    return joined[0], joined[1:]


def backward_layer(dense, experts_pair, saved, grad_low, pack, early, late):
    qkv, out_t, gain_one, shift_one, gain_two, shift_two, router = dense
    first, second = experts_pair[0], experts_pair[1]
    (
        unit_one,
        scale_one,
        normed_one,
        queries,
        keys_all,
        values_all,
        probability,
        prob_low,
        mixed,
        unit_two,
        scale_two,
        normed_two,
        gates,
        table,
        select,
        slot_gates,
        dispatched,
        inner_pre,
        below,
        activated,
        expert_sum,
    ) = saved
    experts = table.shape[0]
    count, width = grad_low.shape
    grad_output = grad_low.astype(F32)
    grad_slots = dot(select, grad_low, ((1,), (0,)))
    slot_chosen = jnp.sum(grad_slots * expert_sum.astype(F32), axis=1).reshape(experts, -1, 1)
    grad_gates = jnp.sum(jnp.where(table, slot_chosen, 0.0), axis=1)
    grad_gates = grad_gates + swap(grad_gates, "mp")
    grad_expert = to_experts(
        (slot_gates * grad_slots).astype(BF16).reshape(experts, -1, width)
    )
    grad_act = dot(grad_expert, second, ((1,), (0,)))
    density = jnp.exp(-0.5 * inner_pre * inner_pre) * (2.0 * 3.141592653589793) ** -0.5
    grad_inner = (grad_act * (below + inner_pre * density)).astype(BF16)
    grad_second = dot(grad_expert, activated, ((0,), (0,))).astype(BF16)
    grad_first = dot(dispatched, grad_inner, ((0,), (0,))).astype(BF16)
    grad_rows = dot(grad_inner, first, ((1,), (1,)))
    grad_dispatched = from_experts(grad_rows, experts)
    pair = jnp.stack([grad_first, grad_second])
    if pack is not None:
        early = early + (pack,)
    corner = pair[:, :8, :128]
    grad_dispatched, (corner, *early) = together(grad_dispatched, (corner,) + early)
    if pack is not None:
        pack = all_to_all(early.pop(), "x")
    expert_grads = lax.psum_scatter(pair, "g", scatter_dimension=1, tiled=True)
    returned = dot(select, grad_dispatched, ((0,), (0,)))
    returned = returned + swap(returned, "mp")
    grad_logits = gates * (grad_gates - jnp.sum(gates * grad_gates, axis=0, keepdims=True))
    grad_router = dot(normed_two.astype(F32), grad_logits, ((0,), (1,)), PRECISE)
    grad_normed = returned + dot(grad_logits, router.astype(F32), ((0,), (1,)), PRECISE)
    grad_hidden, grad_gain_two, grad_shift_two = norm_back(
        grad_normed, unit_two, scale_two, gain_two
    )
    grad_hidden = grad_output + grad_hidden
    blank = jnp.zeros((width, 124), BF16)
    grad_attended = grad_hidden.astype(BF16)
    grad_out_t = dot(grad_attended, mixed, ((0,), (0,)))
    grad_mixed = dot(grad_attended, out_t, ((1,), (0,))).astype(BF16).reshape(queries.shape)
    grad_prob = jnp.einsum("qhe,khe->hqk", grad_mixed, values_all, preferred_element_type=F32)
    grad_values = jnp.einsum("hqk,qhe->khe", prob_low, grad_mixed, preferred_element_type=F32)
    grad_scores = (
        probability * (grad_prob - jnp.sum(probability * grad_prob, axis=-1, keepdims=True))
    ).astype(BF16)
    grad_queries = jnp.einsum(
        "hqk,khe->qhe", grad_scores, keys_all, preferred_element_type=F32
    ) * HEAD_DIM ** (-0.5)
    grad_keys = jnp.einsum(
        "hqk,qhe->khe", grad_scores, queries, preferred_element_type=F32
    ) * HEAD_DIM ** (-0.5)
    grad_projected = (
        jnp.stack([grad_queries, grad_keys, grad_values], axis=1).astype(BF16).reshape(count, -1)
    )
    if pack is not None:
        rest = (grad_out_t, jnp.stack([grad_gain_two, grad_shift_two], axis=1), grad_router)
        rest = jnp.concatenate([part.astype(BF16) for part in rest + (blank[:, 2:],)], axis=1)
        rest, (pack,) = together(by_owner(rest), (pack,))
        rest = all_to_all(rest, "x")
        grad_projected, (rest, *late) = together(grad_projected, (rest,) + late)
    grad_qkv = dot(normed_one, grad_projected, ((0,), (0,)))
    grad_normed = dot(grad_projected, qkv, ((1,), (1,)))
    grad_normed = grad_normed + swap(grad_normed, "mp")
    grad_tokens, grad_gain_one, grad_shift_one = norm_back(
        grad_normed, unit_one, scale_one, gain_one
    )
    ones = jnp.stack([grad_gain_one, grad_shift_one], axis=1)
    if pack is not None:
        dense_grads = (all_to_all(by_owner(grad_qkv), "x"), rest, ones)
    else:
        twos = jnp.stack([grad_gain_two, grad_shift_two], axis=1)
        dense_grads = (grad_qkv, grad_out_t, ones, twos, grad_router, blank[:, 4:])
    grad_low = (grad_hidden + grad_tokens).astype(BF16)
    return grad_low, dense_grads, expert_grads, pack, early, late


def shards(
    inputs,
    cotangent,
    routes,
    gain_one,
    shift_one,
    qkv_weight,
    out_weight,
    gain_two,
    shift_two,
    router,
    expert_in,
    expert_out,
):
    section = lax.axis_index("section")
    mp_index = lax.axis_index("mp")
    size_g = lax.axis_size("g")
    size_x = lax.axis_size("x")
    rows = qkv_weight.shape[1]
    width = rows * size_g * size_x
    half_width = out_weight.shape[1]
    first_section = section == 0

    def by_layer(own):
        other = swap(own, "section")
        return jnp.where(first_section, own, other), jnp.where(first_section, other, own)

    small = jnp.stack([gain_one[0], shift_one[0], gain_two[0], shift_two[0]], axis=1)
    dense_shard = jnp.concatenate(
        [
            qkv_weight[0].reshape(rows, 3 * half_width),
            out_weight[0].T,
            small,
            router[0],
            jnp.zeros((rows, 120), BF16),
        ],
        axis=1,
    )
    expert_shard = jnp.stack([expert_in[0], jnp.swapaxes(expert_out[0], 1, 2)], axis=1)
    routes_own = routes[0, :, 0]
    routes_kept = piece(routes_own, section)
    routes_other = swap(piece(routes_own, 1 - section), "section")
    routes_pair = (
        jnp.where(first_section, routes_kept, routes_other),
        jnp.where(first_section, routes_other, routes_kept),
    )

    full = 3 * half_width

    expert_own = all_to_all(expert_shard, "x")
    expert_own = jnp.swapaxes(expert_own, 0, 1).reshape(2, size_x * rows, -1)
    both = jnp.stack(by_layer(dense_shard))
    both = all_to_all(jnp.broadcast_to(both[None], (size_g,) + both.shape), "g")

    def gathered(layer):
        block = both[:, layer]
        block = all_to_all(jnp.broadcast_to(block[None], (size_x,) + block.shape), "x")
        return jnp.swapaxes(block, 0, 1).reshape(width, -1)

    def dense_weights(pack):
        extra = pack[:, full + half_width : full + half_width + 8]
        vectors = extra[:, :4].astype(F32).T
        return (
            pack[:, :full],
            pack[:, full : full + half_width],
            vectors[0],
            vectors[1],
            vectors[2],
            vectors[3],
            extra[:, 4:],
        )

    own_zero, own_one = by_layer(expert_own)
    pack_zero, (own_one,) = together(gathered(0), (own_one,))
    experts_here = tuple(
        (lax.all_gather(own, "g", axis=1, tiled=True) for own in (own_zero, own_one))
    )
    pack_one = gathered(1)
    dense_zero = dense_weights(pack_zero)
    tables = tuple((slot_table(r, mp_index) for r in routes_pair))
    tokens = piece(inputs[:, 0], section)
    out_zero, saved_zero, pack_one = forward_layer(
        dense_zero, experts_here[0], tokens.astype(F32), tables[0], pack_one
    )
    dense_one = dense_weights(pack_one)
    out_one, saved_one, unused = forward_layer(
        dense_one, experts_here[1], out_zero.astype(F32), tables[1], None
    )

    def traded(zero, one):
        own = jnp.where(first_section, zero, one)
        return own, swap(jnp.where(first_section, one, zero), "section")

    def stacked(own, other):
        low = jnp.where(first_section, own, other)
        high = jnp.where(first_section, other, own)
        return jnp.stack([low, high])[None, :, None]

    acts = stacked(*traded(out_zero, out_one))

    axis_x = lax.axis_index("x")

    def owned_experts(own):
        own = jnp.swapaxes(own.reshape(2, size_x, rows, -1), 0, 1)
        arrived = [piece(own, axis_x)]
        for distance in range(1, size_x):
            arrived.append(swap(piece(own, axis_x ^ distance), "x", distance))
        return xor_order(jnp.stack(arrived), axis_x)

    grad_mid, grads_one, expert_one, unused, (acts,), unused = backward_layer(
        dense_one, experts_here[1], saved_one, piece(cotangent[:, 0], section), None, (acts,), ()
    )
    grad_in, grads_zero, expert_zero, pack_one, unused, late = backward_layer(
        dense_zero,
        experts_here[0],
        saved_zero,
        grad_mid,
        by_owner(jnp.concatenate([part.astype(BF16) for part in grads_one], axis=1)),
        (),
        (owned_experts(expert_one),),
    )
    qkv_zero, rest_zero, ones_zero = grads_zero
    ones_zero = by_owner(ones_zero).reshape(size_x, -1, rows * 2)
    total = piece(ones_zero, axis_x).astype(F32)
    for distance in range(1, size_x):
        arrived = swap(piece(ones_zero, axis_x ^ distance), "x", distance)
        total = total + arrived.astype(F32)
    ones_zero = total.reshape(size_g, rows, 2)
    qkv_zero, rest_zero = summed(qkv_zero), summed(rest_zero)
    dense_zero_sum = jnp.concatenate(
        [
            qkv_zero,
            rest_zero[:, :, :half_width],
            ones_zero,
            rest_zero[:, :, half_width:-2],
        ],
        axis=2,
    )
    dense_both = jnp.stack([dense_zero_sum, summed(pack_one)], axis=1).astype(BF16)
    dense_both = summed(all_to_all(dense_both, "g"))
    dense_own, dense_other = traded(dense_both[0], dense_both[1])
    expert_own, expert_other = traded(owned_experts(expert_zero), late[0])
    grads_own, grads_other = traded(grad_in, grad_mid)
    expert_other, (dense_other, grads_other) = together(expert_other, (dense_other, grads_other))
    input_grads = stacked(grads_own, grads_other)
    dense_sum = dense_own + dense_other
    expert_sum = expert_own.astype(F32) + expert_other.astype(F32)
    grad_first = expert_sum[:, 0]
    grad_second = jnp.swapaxes(expert_sum[:, 1], 1, 2)
    grad_qkv = dense_sum[:, :full].reshape(rows, 3, half_width)
    grad_out = dense_sum[:, full : full + half_width].T
    tail = dense_sum[:, full + half_width :]
    outs = (
        tail[:, 0],
        tail[:, 1],
        grad_qkv,
        grad_out,
        tail[:, 2],
        tail[:, 3],
        tail[:, 4:8],
        grad_first,
        grad_second,
    )
    return (acts, input_grads) + tuple((member[None] for member in outs))


def solution(mesh):
    sections, batch, pair = mesh.devices.shape
    inner = Mesh(mesh.devices.reshape(sections, batch // 4, 4, pair), ("section", "g", "x", "mp"))
    dp = ("g", "x")
    placed = (
        P(None, dp, None, None),
        P(None, dp, None, None),
        P("section", None, dp, None, None),
        P("section", dp),
        P("section", dp),
        P("section", dp, None, "mp"),
        P("section", "mp", dp),
        P("section", dp),
        P("section", dp),
        P("section", dp, None),
        P("section", None, dp, "mp"),
        P("section", None, "mp", dp),
    )
    return jax.shard_map(
        shards,
        mesh=inner,
        in_specs=placed,
        out_specs=(
            P("section", None, dp, None, None),
            P("section", None, dp, None, None),
            P("section", dp),
            P("section", dp),
            P("section", dp, None, "mp"),
            P("section", "mp", dp),
            P("section", dp),
            P("section", dp),
            P("section", dp, None),
            P("section", None, dp, "mp"),
            P("section", None, "mp", dp),
        ),
        check_vma=False,
    )
```

```python
import jax
import jax.numpy as jnp
from jax import lax
from jax.sharding import Mesh
from jax.sharding import PartitionSpec as P

HEAD_DIM = 64
SEQ = 197
CAP = 128
EPS = 1e-06
PRECISE = lax.Precision.HIGHEST
F32 = jnp.float32
BF16 = jnp.bfloat16


def dot(a, b, dims, precision=None):
    return lax.dot_general(a, b, (dims, ((), ())), precision=precision, preferred_element_type=F32)


def swap(block, axis, distance=1):
    size = lax.axis_size(axis)
    return lax.ppermute(block, axis, [(i, i ^ distance) for i in range(size)])


def piece(blocks, index):
    return lax.dynamic_index_in_dim(blocks, index, 0, keepdims=False)


def all_to_all(blocks, axis):
    return lax.all_to_all(blocks, axis, 0, 0, tiled=True)


def summed(blocks):
    return jnp.sum(blocks.astype(F32), axis=0)


def xor_order(blocks, index):
    paired = blocks.reshape((2, 2) + blocks.shape[1:])
    paired = jnp.where((index & 1) == 1, paired[:, ::-1], paired)
    paired = jnp.where((index & 2) == 2, paired[::-1], paired)
    return paired.reshape(blocks.shape)


def by_owner(grad):
    size_g, size_x = lax.axis_size("g"), lax.axis_size("x")
    blocks = grad.astype(BF16).reshape(size_g, size_x, -1, grad.shape[1])
    return jnp.swapaxes(blocks, 0, 1)


def normalise(field):
    centered = field - jnp.mean(field, axis=-1, keepdims=True)
    scale = lax.rsqrt(jnp.mean(centered * centered, axis=-1, keepdims=True) + EPS)
    return centered * scale, scale


def norm_back(grad, unit, scale, gain):
    grad_unit = grad * gain[None, :]
    mean_grad = jnp.mean(grad_unit, axis=-1, keepdims=True)
    mean_cross = jnp.mean(grad_unit * unit, axis=-1, keepdims=True)
    grad_field = scale * (grad_unit - mean_grad - unit * mean_cross)
    return grad_field, jnp.sum(grad * unit, axis=0), jnp.sum(grad, axis=0)


def slot_table(route_ids, mp_index):
    tokens = route_ids.shape[0]
    order = jnp.arange(lax.axis_size("x"), dtype=jnp.int32)
    named = jnp.any(route_ids.T[None, :, :] == order[:, None, None], axis=1)
    steps = jnp.arange(tokens, dtype=jnp.int32)
    earlier = (steps[:, None] < steps[None, :]).astype(BF16)
    position = dot(named.astype(BF16), earlier, ((1,), (0,))).astype(jnp.int32)
    slots = jnp.arange(CAP // 2, dtype=jnp.int32) + mp_index * (CAP // 2)
    return named[:, None, :] & (position[:, None, :] == slots[None, :, None])


def to_experts(half):
    own = all_to_all(half, "x").reshape(-1, half.shape[2])
    return jnp.concatenate([own, swap(own, "mp")], axis=0)


def from_experts(partial, experts):
    rows = partial.shape[0] // 2
    other = swap(partial[rows:].astype(BF16), "mp")
    own = (partial[:rows] + other.astype(F32)).astype(BF16)
    own = own.reshape(experts, rows // experts, -1)
    return all_to_all(own, "x").reshape(rows, -1)


def forward_layer(dense, experts_pair, tokens, table, beside):
    qkv, out_t, gain_one, shift_one, gain_two, shift_two, router = dense
    first, second = experts_pair[0], experts_pair[1]
    count, width = tokens.shape
    experts = table.shape[0]
    half_width = out_t.shape[1]
    heads = half_width // HEAD_DIM
    unit_one, scale_one = normalise(tokens)
    normed_one = (unit_one * gain_one[None, :] + shift_one[None, :]).astype(BF16)
    projected = dot(normed_one, qkv, ((1,), (0,))).astype(BF16)
    parts = projected.reshape(count, 3, heads, HEAD_DIM)
    queries, keys_all, values_all = parts[:, 0], parts[:, 1], parts[:, 2]
    scores = jnp.einsum(
        "qhe,khe->hqk", queries, keys_all, preferred_element_type=F32
    ) * HEAD_DIM ** (-0.5)
    probability = jax.nn.softmax(scores, axis=-1)
    prob_low = probability.astype(BF16)
    mixed = (
        jnp.einsum("hqk,khe->qhe", prob_low, values_all, preferred_element_type=F32)
        .astype(BF16)
        .reshape(count, half_width)
    )
    attended = dot(mixed, out_t, ((1,), (1,)))
    attended = attended + swap(attended, "mp")
    hidden = tokens + attended
    unit_two, scale_two = normalise(hidden)
    normed_two = (unit_two * gain_two[None, :] + shift_two[None, :]).astype(BF16)
    gates = jax.nn.softmax(dot(router, normed_two, ((0,), (1,))), axis=0)
    select = table.astype(BF16).reshape(-1, count)
    slot_gates = jnp.sum(jnp.where(table, gates[:, None, :], 0.0), axis=2).reshape(-1, 1)
    dispatched = to_experts(
        dot(select, normed_two, ((1,), (0,))).astype(BF16).reshape(experts, -1, width)
    )
    if beside is not None:
        dispatched, beside = lax.optimization_barrier((dispatched, beside))
    inner_pre = dot(dispatched, first, ((1,), (0,)))
    below = 0.5 * (1.0 + lax.erf(inner_pre * 0.5**0.5))
    activated = (inner_pre * below).astype(BF16)
    expert_sum = from_experts(dot(activated, second, ((1,), (1,))), experts)
    weighted = (slot_gates * expert_sum.astype(F32)).astype(BF16)
    mixture = dot(select, weighted, ((0,), (0,)))
    output = hidden + (mixture + swap(mixture, "mp"))
    saved = (
        unit_one,
        scale_one,
        normed_one,
        queries,
        keys_all,
        values_all,
        probability,
        prob_low,
        mixed,
        unit_two,
        scale_two,
        normed_two,
        gates,
        table,
        select,
        slot_gates,
        dispatched,
        inner_pre,
        below,
        activated,
        expert_sum,
    )
    return output.astype(BF16), saved, beside


def together(value, others):
    joined = lax.optimization_barrier((value,) + tuple(others))
    return joined[0], joined[1:]


def backward_layer(dense, experts_pair, saved, grad_low, pack, early, late):
    qkv, out_t, gain_one, shift_one, gain_two, shift_two, router = dense
    first, second = experts_pair[0], experts_pair[1]
    (
        unit_one,
        scale_one,
        normed_one,
        queries,
        keys_all,
        values_all,
        probability,
        prob_low,
        mixed,
        unit_two,
        scale_two,
        normed_two,
        gates,
        table,
        select,
        slot_gates,
        dispatched,
        inner_pre,
        below,
        activated,
        expert_sum,
    ) = saved
    experts = table.shape[0]
    count, width = grad_low.shape
    grad_output = grad_low.astype(F32)
    grad_slots = dot(select, grad_low, ((1,), (0,)))
    slot_chosen = jnp.sum(grad_slots * expert_sum.astype(F32), axis=1).reshape(experts, -1, 1)
    grad_gates = jnp.sum(jnp.where(table, slot_chosen, 0.0), axis=1)
    grad_gates = grad_gates + swap(grad_gates, "mp")
    grad_expert = to_experts(
        (slot_gates * grad_slots).astype(BF16).reshape(experts, -1, width)
    )
    grad_act = dot(grad_expert, second, ((1,), (0,)))
    density = jnp.exp(-0.5 * inner_pre * inner_pre) * (2.0 * 3.141592653589793) ** -0.5
    grad_inner = (grad_act * (below + inner_pre * density)).astype(BF16)
    grad_second = dot(grad_expert, activated, ((0,), (0,))).astype(BF16)
    grad_first = dot(dispatched, grad_inner, ((0,), (0,))).astype(BF16)
    grad_rows = dot(grad_inner, first, ((1,), (1,)))
    grad_dispatched = from_experts(grad_rows, experts)
    pair = jnp.stack([grad_first, grad_second])
    if pack is not None:
        early = early + (pack,)
    corner = pair[:, :8, :128]
    grad_dispatched, (corner, *early) = together(grad_dispatched, (corner,) + early)
    if pack is not None:
        pack = all_to_all(early.pop(), "x")
    expert_grads = lax.psum_scatter(pair, "g", scatter_dimension=1, tiled=True)
    returned = dot(select, grad_dispatched, ((0,), (0,)))
    returned = returned + swap(returned, "mp")
    grad_logits = gates * (grad_gates - jnp.sum(gates * grad_gates, axis=0, keepdims=True))
    grad_router = dot(normed_two.astype(F32), grad_logits, ((0,), (1,)), PRECISE)
    grad_normed = returned + dot(grad_logits, router.astype(F32), ((0,), (1,)), PRECISE)
    grad_hidden, grad_gain_two, grad_shift_two = norm_back(
        grad_normed, unit_two, scale_two, gain_two
    )
    grad_hidden = grad_output + grad_hidden
    blank = jnp.zeros((width, 124), BF16)
    grad_attended = grad_hidden.astype(BF16)
    grad_out_t = dot(grad_attended, mixed, ((0,), (0,)))
    grad_mixed = dot(grad_attended, out_t, ((1,), (0,))).astype(BF16).reshape(queries.shape)
    grad_prob = jnp.einsum("qhe,khe->hqk", grad_mixed, values_all, preferred_element_type=F32)
    grad_values = jnp.einsum("hqk,qhe->khe", prob_low, grad_mixed, preferred_element_type=F32)
    grad_scores = (
        probability * (grad_prob - jnp.sum(probability * grad_prob, axis=-1, keepdims=True))
    ).astype(BF16)
    grad_queries = jnp.einsum(
        "hqk,khe->qhe", grad_scores, keys_all, preferred_element_type=F32
    ) * HEAD_DIM ** (-0.5)
    grad_keys = jnp.einsum(
        "hqk,qhe->khe", grad_scores, queries, preferred_element_type=F32
    ) * HEAD_DIM ** (-0.5)
    grad_projected = (
        jnp.stack([grad_queries, grad_keys, grad_values], axis=1).astype(BF16).reshape(count, -1)
    )
    if pack is not None:
        rest = (grad_out_t, jnp.stack([grad_gain_two, grad_shift_two], axis=1), grad_router)
        rest = jnp.concatenate([part.astype(BF16) for part in rest + (blank[:, 2:],)], axis=1)
        rest, (pack,) = together(by_owner(rest), (pack,))
        rest = all_to_all(rest, "x")
        grad_projected, (rest, *late) = together(grad_projected, (rest,) + late)
    grad_qkv = dot(normed_one, grad_projected, ((0,), (0,)))
    grad_normed = dot(grad_projected, qkv, ((1,), (1,)))
    grad_normed = grad_normed + swap(grad_normed, "mp")
    grad_tokens, grad_gain_one, grad_shift_one = norm_back(
        grad_normed, unit_one, scale_one, gain_one
    )
    ones = jnp.stack([grad_gain_one, grad_shift_one], axis=1)
    if pack is not None:
        dense_grads = (all_to_all(by_owner(grad_qkv), "x"), rest, ones)
    else:
        twos = jnp.stack([grad_gain_two, grad_shift_two], axis=1)
        dense_grads = (grad_qkv, grad_out_t, ones, twos, grad_router, blank[:, 4:])
    grad_low = (grad_hidden + grad_tokens).astype(BF16)
    return grad_low, dense_grads, expert_grads, pack, early, late


def shards(
    inputs,
    cotangent,
    routes,
    gain_one,
    shift_one,
    qkv_weight,
    out_weight,
    gain_two,
    shift_two,
    router,
    expert_in,
    expert_out,
):
    section = lax.axis_index("section")
    mp_index = lax.axis_index("mp")
    size_g = lax.axis_size("g")
    size_x = lax.axis_size("x")
    rows = qkv_weight.shape[1]
    width = rows * size_g * size_x
    half_width = out_weight.shape[1]
    first_section = section == 0

    def by_layer(own):
        other = swap(own, "section")
        return jnp.where(first_section, own, other), jnp.where(first_section, other, own)

    small = jnp.stack([gain_one[0], shift_one[0], gain_two[0], shift_two[0]], axis=1)
    dense_shard = jnp.concatenate(
        [
            qkv_weight[0].reshape(rows, 3 * half_width),
            out_weight[0].T,
            small,
            router[0],
            jnp.zeros((rows, 120), BF16),
        ],
        axis=1,
    )
    expert_shard = jnp.stack([expert_in[0], jnp.swapaxes(expert_out[0], 1, 2)], axis=1)
    routes_own = routes[0, :, 0]
    routes_kept = piece(routes_own, section)
    routes_other = swap(piece(routes_own, 1 - section), "section")
    routes_pair = (
        jnp.where(first_section, routes_kept, routes_other),
        jnp.where(first_section, routes_other, routes_kept),
    )

    full = 3 * half_width

    expert_own = all_to_all(expert_shard, "x")
    expert_own = jnp.swapaxes(expert_own, 0, 1).reshape(2, size_x * rows, -1)
    both = jnp.stack(by_layer(dense_shard))
    both = all_to_all(jnp.broadcast_to(both[None], (size_g,) + both.shape), "g")

    def gathered(layer):
        block = both[:, layer]
        block = all_to_all(jnp.broadcast_to(block[None], (size_x,) + block.shape), "x")
        return jnp.swapaxes(block, 0, 1).reshape(width, -1)

    def dense_weights(pack):
        extra = pack[:, full + half_width : full + half_width + 8]
        vectors = extra[:, :4].astype(F32).T
        return (
            pack[:, :full],
            pack[:, full : full + half_width],
            vectors[0],
            vectors[1],
            vectors[2],
            vectors[3],
            extra[:, 4:],
        )

    own_zero, own_one = by_layer(expert_own)
    pack_zero, (own_one,) = together(gathered(0), (own_one,))
    experts_here = tuple(
        (lax.all_gather(own, "g", axis=1, tiled=True) for own in (own_zero, own_one))
    )
    pack_one = gathered(1)
    dense_zero = dense_weights(pack_zero)
    tables = tuple((slot_table(r, mp_index) for r in routes_pair))
    tokens = piece(inputs[:, 0], section)
    out_zero, saved_zero, pack_one = forward_layer(
        dense_zero, experts_here[0], tokens.astype(F32), tables[0], pack_one
    )
    dense_one = dense_weights(pack_one)
    out_one, saved_one, unused = forward_layer(
        dense_one, experts_here[1], out_zero.astype(F32), tables[1], None
    )

    def traded(zero, one):
        own = jnp.where(first_section, zero, one)
        return own, swap(jnp.where(first_section, one, zero), "section")

    def stacked(own, other):
        low = jnp.where(first_section, own, other)
        high = jnp.where(first_section, other, own)
        return jnp.stack([low, high])[None, :, None]

    acts = stacked(*traded(out_zero, out_one))

    axis_x = lax.axis_index("x")

    def owned_experts(own):
        own = jnp.swapaxes(own.reshape(2, size_x, rows, -1), 0, 1)
        arrived = [piece(own, axis_x)]
        for distance in range(1, size_x):
            arrived.append(swap(piece(own, axis_x ^ distance), "x", distance))
        return tuple(arrived)

    grad_mid, grads_one, expert_one, unused, (acts,), unused = backward_layer(
        dense_one, experts_here[1], saved_one, piece(cotangent[:, 0], section), None, (acts,), ()
    )
    grad_in, grads_zero, expert_zero, pack_one, unused, late = backward_layer(
        dense_zero,
        experts_here[0],
        saved_zero,
        grad_mid,
        by_owner(jnp.concatenate([part.astype(BF16) for part in grads_one], axis=1)),
        (),
        owned_experts(expert_one),
    )
    qkv_zero, rest_zero, ones_zero = grads_zero
    ones_zero = by_owner(ones_zero).reshape(size_x, -1, rows * 2)
    total = piece(ones_zero, axis_x).astype(F32)
    for distance in range(1, size_x):
        arrived = swap(piece(ones_zero, axis_x ^ distance), "x", distance)
        total = total + arrived.astype(F32)
    ones_zero = total.reshape(size_g, rows, 2)
    qkv_zero, rest_zero = summed(qkv_zero), summed(rest_zero)
    dense_zero_sum = jnp.concatenate(
        [
            qkv_zero,
            rest_zero[:, :, :half_width],
            ones_zero,
            rest_zero[:, :, half_width:-2],
        ],
        axis=2,
    )
    dense_both = jnp.stack([dense_zero_sum, summed(pack_one)], axis=1).astype(BF16)
    dense_both = summed(all_to_all(dense_both, "g"))
    dense_own, dense_other = traded(dense_both[0], dense_both[1])
    pairs = [traded(zero, one) for zero, one in zip(owned_experts(expert_zero), late)]
    expert_own, expert_other = (xor_order(jnp.stack(side), axis_x) for side in zip(*pairs))
    grads_own, grads_other = traded(grad_in, grad_mid)
    expert_other, (dense_other, grads_other) = together(expert_other, (dense_other, grads_other))
    input_grads = stacked(grads_own, grads_other)
    dense_sum = dense_own + dense_other
    expert_sum = expert_own.astype(F32) + expert_other.astype(F32)
    grad_first = expert_sum[:, 0]
    grad_second = jnp.swapaxes(expert_sum[:, 1], 1, 2)
    grad_qkv = dense_sum[:, :full].reshape(rows, 3, half_width)
    grad_out = dense_sum[:, full : full + half_width].T
    tail = dense_sum[:, full + half_width :]
    outs = (
        tail[:, 0],
        tail[:, 1],
        grad_qkv,
        grad_out,
        tail[:, 2],
        tail[:, 3],
        tail[:, 4:8],
        grad_first,
        grad_second,
    )
    return (acts, input_grads) + tuple((member[None] for member in outs))


def solution(mesh):
    sections, batch, pair = mesh.devices.shape
    inner = Mesh(mesh.devices.reshape(sections, batch // 4, 4, pair), ("section", "g", "x", "mp"))
    dp = ("g", "x")
    placed = (
        P(None, dp, None, None),
        P(None, dp, None, None),
        P("section", None, dp, None, None),
        P("section", dp),
        P("section", dp),
        P("section", dp, None, "mp"),
        P("section", "mp", dp),
        P("section", dp),
        P("section", dp),
        P("section", dp, None),
        P("section", None, dp, "mp"),
        P("section", None, "mp", dp),
    )
    return jax.shard_map(
        shards,
        mesh=inner,
        in_specs=placed,
        out_specs=(
            P("section", None, dp, None, None),
            P("section", None, dp, None, None),
            P("section", dp),
            P("section", dp),
            P("section", dp, None, "mp"),
            P("section", "mp", dp),
            P("section", dp),
            P("section", dp),
            P("section", dp, None),
            P("section", None, dp, "mp"),
            P("section", None, "mp", dp),
        ),
        check_vma=False,
    )
```
